128 devices in a mesh: dp: 16 (over z, y), tensor: 8 (over x, core).
Axes of the slice: x: 4, y: 4, z: 4, core: 2. Of those that a mesh axis runs over, the one named last changes fastest.
Arguments:
- tokens: bfloat16 [32768, 8192], P('dp', 'tensor'), may hold values from -6 to 6
- cotangent: bfloat16 [32768, 1024], P('dp', 'tensor'), may hold values from -6 to 6
- value_matrix: bfloat16 [8192, 1024], P('tensor'), may hold values from -0.0625 to 0.0625
- down_factors: bfloat16 [256, 8192, 64], P('dp', 'tensor'), may hold values from -0.0625 to 0.0625
- up_factors: bfloat16 [256, 64, 1024], P('dp', None, 'tensor'), may hold values from -0.75 to 0.75
- tile_usage_entry: int32 [256], P('dp'), may hold values from 0 to 7, as said below
- usage: int32 [128], replicated, may hold values from 0 to 255, as said below
- storage_row_map: int32 [256], replicated, may hold values from 0 to 255, as said below
Outputs:
- projected: bfloat16 [32768, 1024], P('dp', 'tensor')
- input_gradient: bfloat16 [32768, 8192], P('dp', 'tensor')
- down_gradient: bfloat16 [256, 8192, 64], P('dp', 'tensor')
- up_gradient: bfloat16 [256, 64, 1024], P('dp', None, 'tensor')
The draws below stay inside these ranges and needn't reach their ends.
Inputs may be any that keep to these rules, and one draw needn't show every extreme that they name: `tile_usage_entry`: each dp index's 256 / 16 entries name every one of its 8 list entries. `usage`: the 8 ids of one dp index are stored (storage_row_map) on 8 different dp indices, storage row // 16. `storage_row_map`: A permutation.
All inputs are finite; a program needn't handle non-finite values.
Results may differ from the reference program's by a relative error of at most 0.02.
Values may be sent and summed in bfloat16 or wider, within the bound.
No kernel may reach another device: no remote copies, remote signals or barrier semaphores. Data moves between devices by JAX's collectives and lax.ppermute only.
A program may use at most 128 MiB of HBM per device.

```python
import jax
import jax.numpy as jnp
from jax import lax

MODEL_WIDTH = 8192
VALUE_WIDTH = 1024
ADAPTER_RANK = 64
ADAPTER_TOTAL = 256
U = 8
TILE = 128
TOKEN_ROWS_SHARD = 2048
TOKENS = 32768
N_DP = 16
N_TENSOR = 8


def storage_order(key):
    return jax.random.permutation(key, ADAPTER_TOTAL).astype(jnp.int32)


def owner_pick(subkey):
    return jax.random.permutation(subkey, N_DP)[:U]


def row_shuffle(subkey, values):
    return jax.random.permutation(subkey, values)


def draw_storage_row_map(key, part):
    shared = storage_order(key)
    return shared.astype(jnp.int32)


def draw_usage(key, part):
    shared = storage_order(key)
    key = jax.random.fold_in(key, 12)
    keys = jax.random.split(key, N_DP + 1)
    owners = jax.vmap(owner_pick)(keys[:N_DP]).astype(jnp.int32)
    local_rows = jax.random.randint(keys[N_DP], (N_DP, U), 0, ADAPTER_TOTAL // N_DP).astype(jnp.int32)
    storage = owners * (ADAPTER_TOTAL // N_DP) + local_rows
    inverse = jnp.argsort(shared, stable=True).astype(jnp.int32)
    return jnp.take(inverse, storage.reshape(-1)).astype(jnp.int32)


def draw_tile_usage_entry(key, part):
    key = jax.random.fold_in(key, 13)
    extra_key, order_key = jax.random.split(key)
    extra = jax.random.randint(extra_key, (N_DP, TOKEN_ROWS_SHARD // TILE - U), 0, U).astype(jnp.int32)
    every_slot = jnp.broadcast_to(jnp.arange(U, dtype=jnp.int32)[None, :], (N_DP, U))
    joined = jnp.concatenate([every_slot, extra], axis=1)
    order_keys = jax.random.split(order_key, N_DP)
    shuffled = jax.vmap(row_shuffle)(order_keys, joined)
    return shuffled.reshape(-1).astype(jnp.int32)


def level_of(stream_key, dims, pieces, low, top_value):
    factor_of, own = 1.0, jax.random.fold_in(stream_key, 6)
    for dim, parts in pieces:
        draws = jnp.exp(jax.random.uniform(jax.random.fold_in(own, dim), (parts,), jnp.float32, low / len(pieces), top_value / len(pieces)))
        factor_of = factor_of * jnp.repeat(draws, dims[dim] // parts).reshape([-1 if axis == dim else 1 for axis in range(len(dims))])
    return factor_of


def noise(own_key, dims, spread, bound, cuts=(), held_as=jnp.bfloat16):
    entries = spread * jax.random.normal(own_key, dims, jnp.float32)
    if cuts:
        entries = entries * level_of(own_key, dims, cuts, -0.22, 0.18)
    return jnp.clip(entries, -bound, bound).astype(held_as)


def setup_inputs(seed: int = 0) -> dict:
    streams_of = jax.random.split(jax.random.key(seed), 9)
    return {
        "tokens": noise(streams_of[0], (TOKENS, MODEL_WIDTH), 1.0, 6.0, ((0, 16), (1, 8))),
        "cotangent": noise(streams_of[1], (TOKENS, VALUE_WIDTH), 1.0, 6.0, ((0, 16), (1, 8))),
        "value_matrix": noise(streams_of[2], (MODEL_WIDTH, VALUE_WIDTH), MODEL_WIDTH ** -0.5, 0.0625, ((0, 8),)),
        "down_factors": noise(streams_of[3], (ADAPTER_TOTAL, MODEL_WIDTH, ADAPTER_RANK), MODEL_WIDTH ** -0.5, 0.0625, ((0, 16), (1, 8))),
        "up_factors": noise(streams_of[4], (ADAPTER_TOTAL, ADAPTER_RANK, VALUE_WIDTH), ADAPTER_RANK ** -0.5, 0.75, ((0, 16), (2, 8))),
        "tile_usage_entry": draw_tile_usage_entry(jax.random.fold_in(streams_of[8], 71), 0),
        "usage": draw_usage(jax.random.fold_in(streams_of[8], 71), 0),
        "storage_row_map": draw_storage_row_map(jax.random.fold_in(streams_of[8], 71), 0),
    }


ADAPTER_SCALE = 2.0


def reference(tokens, cotangent, value_matrix, down_factors, up_factors, tile_usage_entry, usage, storage_row_map):
    tiles_number_count = TOKEN_ROWS_SHARD // TILE
    block = MODEL_WIDTH // N_TENSOR
    xs = tokens.reshape(N_DP, TOKEN_ROWS_SHARD, MODEL_WIDTH)
    dys = cotangent.reshape(N_DP, TOKEN_ROWS_SHARD, VALUE_WIDTH)
    tiles = tile_usage_entry.reshape(N_DP, tiles_number_count)
    usages = usage.reshape(N_DP, U)
    init = (jnp.zeros((ADAPTER_TOTAL, MODEL_WIDTH, ADAPTER_RANK), jnp.float32), jnp.zeros((ADAPTER_TOTAL, ADAPTER_RANK, VALUE_WIDTH), jnp.float32))

    def step(carry, inputs):
        x_group, dy_group, tile_group, usage_group = inputs
        adapters = jnp.take(usage_group, tile_group).astype(jnp.int32)
        token_rows = jnp.take(storage_row_map, adapters).astype(jnp.int32)
        tile_down_factor = jnp.take(down_factors, token_rows, axis=0).astype(jnp.float32)
        tile_up_factor = jnp.take(up_factors, token_rows, axis=0).astype(jnp.float32)
        x_tiles = x_group.reshape(tiles_number_count, TILE, MODEL_WIDTH).astype(jnp.float32)
        dy_tiles = dy_group.reshape(tiles_number_count, TILE, VALUE_WIDTH).astype(jnp.float32)
        lowrank = jnp.einsum("tnd,tdr->tnr", x_tiles, tile_down_factor).astype(jnp.bfloat16)
        narrow_broad = lowrank.astype(jnp.float32)
        frozen_output = jnp.zeros((TOKEN_ROWS_SHARD, VALUE_WIDTH), jnp.float32)
        for index in range(N_TENSOR):
            partial_sum = jnp.dot(x_group[:, index * block:(index + 1) * block],
                                  value_matrix[index * block:(index + 1) * block],
                                  preferred_element_type=jnp.float32).astype(jnp.bfloat16)
            frozen_output = frozen_output + lax.optimization_barrier(partial_sum).astype(jnp.float32)
        adapter_output = jnp.einsum("wym,wmi->wyi", narrow_broad, tile_up_factor).reshape(TOKEN_ROWS_SHARD, VALUE_WIDTH)
        projected = (frozen_output + ADAPTER_SCALE * adapter_output).astype(jnp.bfloat16)
        back_low = jnp.einsum("tnk,trk->tnr", dy_tiles, tile_up_factor).astype(jnp.bfloat16)
        backward_broad = back_low.astype(jnp.float32)
        frozen_share = jnp.dot(dy_group, value_matrix.T, preferred_element_type=jnp.float32)
        adapter_backward = jnp.einsum("qou,qyu->qoy", backward_broad, tile_down_factor).reshape(TOKEN_ROWS_SHARD, MODEL_WIDTH)
        input_gradient = (frozen_share + ADAPTER_SCALE * adapter_backward).astype(jnp.bfloat16)
        grad_tiles_a = jnp.einsum("tnd,tnr->tdr", x_tiles, backward_broad)
        grad_tiles_b = jnp.einsum("tnr,tnk->trk", narrow_broad, dy_tiles)
        carry = (carry[0].at[token_rows].add(grad_tiles_a), carry[1].at[token_rows].add(grad_tiles_b))
        return carry, (projected, input_gradient)

    (down_total_sum, up_total_sum), (projected, input_gradient) = lax.scan(step, init, (xs, dys, tiles, usages))
    down_gradient = (ADAPTER_SCALE * down_total_sum).astype(jnp.bfloat16)
    up_gradient = (ADAPTER_SCALE * up_total_sum).astype(jnp.bfloat16)
    return projected.reshape(TOKENS, VALUE_WIDTH), input_gradient.reshape(TOKENS, MODEL_WIDTH), down_gradient, up_gradient
```

```python
import jax
import jax.numpy as jnp
from jax import lax
from jax.experimental import pallas as pl
from jax.experimental.pallas import tpu as pltpu
from jax.sharding import PartitionSpec as P

TILE = 128
ADAPTER_SCALE = 2.0
F32 = jnp.float32
BF16 = jnp.bfloat16
ANY = pl.BlockSpec(memory_space=pl.ANY)
SMEM = pl.BlockSpec(memory_space=pltpu.SMEM)
VMEM = pl.BlockSpec(memory_space=pltpu.VMEM)
LIMIT = 48 * 1024 * 1024


def dot(a, b, contract):
    return lax.dot_general(a, b, ((contract[:1], contract[1:]), ((), ())), preferred_element_type=F32)


def cost(flops, nbytes):
    return pl.CostEstimate(flops=flops, bytes_accessed=nbytes, transcendentals=0)


def params():
    return pltpu.CompilerParams(vmem_limit_bytes=LIMIT)


def copy_rows(rows, source, target, sems):
    count = target.shape[0]
    copies = []
    for user in range(count):
        row = jnp.maximum(rows[user], 0)
        copies.append(pltpu.make_async_copy(source.at[row], target.at[user], sems.at[user]))
        copies[-1].start()
    for copy in copies:
        copy.wait()


def route_up(me, usage, storage_row_map, entries, up, holding):
    users = usage.shape[0] // 8
    tiles = entries.shape[0]

    def kernel(me_ref, usage_ref, map_ref, entry_ref, up_ref, rows_ref, holders_ref, send_ref, sems):
        mine = me_ref[0]
        for user in range(users):
            row = jnp.int32(-1)
            for slot in range(8):
                place = map_ref[usage_ref[user * 8 + slot]]
                row = jnp.where(place // holding == mine, place % holding, row)
            rows_ref[user] = row
        for tile in range(tiles):
            holders_ref[tile] = map_ref[usage_ref[mine * 8 + entry_ref[tile]]] // holding
        copy_rows(rows_ref, up_ref, send_ref, sems)

    return pl.pallas_call(
        kernel,
        out_shape=(
            jax.ShapeDtypeStruct((users,), jnp.int32),
            jax.ShapeDtypeStruct((tiles,), jnp.int32),
            jax.ShapeDtypeStruct((users,) + up.shape[1:], BF16),
        ),
        in_specs=[SMEM, SMEM, SMEM, SMEM, ANY],
        out_specs=(SMEM, SMEM, ANY),
        scratch_shapes=[pltpu.SemaphoreType.DMA((users,))],
        compiler_params=params(),
        cost_estimate=cost(0, 2 * up.size * 2),
        name="route_up",
    )(me, usage, storage_row_map, entries, up)


def select_rows(rows, stored):
    users = rows.shape[0]
    return pl.pallas_call(
        copy_rows,
        out_shape=jax.ShapeDtypeStruct((users,) + stored.shape[1:], BF16),
        in_specs=[SMEM, ANY],
        out_specs=ANY,
        scratch_shapes=[pltpu.SemaphoreType.DMA((users,))],
        compiler_params=params(),
        cost_estimate=cost(0, 2 * stored.size * 2),
        name="select_down",
    )(rows, stored)


def base_product(tokens, value_matrix, shards_number):
    rows, features = tokens.shape
    columns = value_matrix.shape[1]
    width = columns // shards_number
    block = 512

    def kernel(x_ref, v_ref, o_ref):
        product = dot(x_ref[...], v_ref[...], (1, 0))
        for index in range(shards_number):
            o_ref[index] = product[:, index * width : (index + 1) * width].astype(BF16)

    return pl.pallas_call(
        kernel,
        grid=(rows // block,),
        out_shape=jax.ShapeDtypeStruct((shards_number, rows, width), BF16),
        in_specs=[
            pl.BlockSpec((block, features), lambda i: (i, 0)),
            pl.BlockSpec((features, columns), lambda i: (0, 0)),
        ],
        out_specs=pl.BlockSpec((shards_number, block, width), lambda i: (0, i, 0)),
        compiler_params=params(),
        cost_estimate=cost(2 * rows * features * columns, 2 * (rows * features + features * columns + rows * columns)),
        name="base_product",
    )(tokens, value_matrix)


def back_product(holders, up, cotangent):
    tiles = holders.shape[0]

    def kernel(h_ref, up_ref, dy_ref, o_ref):
        for tile in range(tiles):
            o_ref[tile] = dot(
                up_ref[h_ref[tile]], dy_ref[tile * TILE : (tile + 1) * TILE, :], (1, 1)
            ).astype(BF16)

    return pl.pallas_call(
        kernel,
        out_shape=jax.ShapeDtypeStruct((tiles, up.shape[1], TILE), BF16),
        in_specs=[SMEM, VMEM, VMEM],
        out_specs=VMEM,
        compiler_params=params(),
        cost_estimate=cost(2 * cotangent.size * up.shape[1], 2 * 3 * cotangent.size),
        name="back_product",
    )(holders, up, cotangent)


def low_product(holders, down, tokens):
    tiles = holders.shape[0]
    rows, features = tokens.shape
    rank = down.shape[1]
    group = 4

    def kernel(h_ref, down_ref, x_ref, o_ref):
        first = pl.program_id(0) * group
        for tile in range(group):
            o_ref[tile] = dot(
                down_ref[h_ref[first + tile]], x_ref[tile * TILE : (tile + 1) * TILE, :], (1, 1)
            ).astype(BF16)

    return pl.pallas_call(
        kernel,
        grid=(tiles // group,),
        out_shape=jax.ShapeDtypeStruct((tiles, rank, TILE), BF16),
        in_specs=[
            SMEM,
            pl.BlockSpec(down.shape, lambda i: (0, 0, 0)),
            pl.BlockSpec((group * TILE, features), lambda i: (i, 0)),
        ],
        out_specs=pl.BlockSpec((group, rank, TILE), lambda i: (i, 0, 0)),
        compiler_params=params(),
        cost_estimate=cost(8 * tokens.size * rank, 2 * (tokens.size + down.size)),
        name="low_product",
    )(holders, down, tokens)


def gradient_terms(holders, rank_side, wide_side, owners, step):
    tiles, rank, _ = rank_side.shape
    rows, width = wide_side.shape

    def kernel(h_ref, r_ref, w_ref, o_ref, total):
        total[...] = jnp.zeros_like(total)
        for tile in range(tiles):
            total[h_ref[tile]] += dot(r_ref[tile], w_ref[tile * TILE : (tile + 1) * TILE, :], (1, 0))
        o_ref[...] = (ADAPTER_SCALE * total[...]).astype(BF16)

    return pl.pallas_call(
        kernel,
        grid=(width // step,),
        out_shape=jax.ShapeDtypeStruct((owners, rank, width), BF16),
        in_specs=[
            SMEM,
            pl.BlockSpec(rank_side.shape, lambda i: (0, 0, 0)),
            pl.BlockSpec((rows, step), lambda i: (0, i)),
        ],
        out_specs=pl.BlockSpec((owners, rank, step), lambda i: (0, 0, i)),
        scratch_shapes=[pltpu.VMEM((owners, rank, step), F32)],
        compiler_params=params(),
        cost_estimate=cost(8 * wide_side.size * rank, 2 * (wide_side.size + owners * rank * width)),
        name="gradient_terms",
    )(holders, rank_side, wide_side)


def combine(rows, received, holding, step):
    users, rank, width = received.shape

    def kernel(rows_ref, r_ref, o_ref, total):
        total[...] = jnp.zeros_like(total)
        for user in range(users):

            @pl.when(rows_ref[user] >= 0)
            def _():
                total[jnp.maximum(rows_ref[user], 0)] += r_ref[user].astype(F32)

        o_ref[...] = total[...].astype(BF16)

    return pl.pallas_call(
        kernel,
        grid=(width // step,),
        out_shape=jax.ShapeDtypeStruct((holding, rank, width), BF16),
        in_specs=[SMEM, pl.BlockSpec((users, rank, step), lambda i: (0, 0, i))],
        out_specs=pl.BlockSpec((holding, rank, step), lambda i: (0, 0, i)),
        scratch_shapes=[pltpu.VMEM((holding, rank, step), F32)],
        compiler_params=params(),
        cost_estimate=cost(4 * received.size, 4 * received.size),
        name="combine",
    )(rows, received)


def finish_projected(holders, frozen, lowrank, up):
    tiles = holders.shape[0]

    def kernel(h_ref, f_ref, l_ref, up_ref, o_ref):
        for tile in range(tiles):
            span = slice(tile * TILE, (tile + 1) * TILE)
            adapter = dot(l_ref[tile], up_ref[h_ref[tile]], (0, 0))
            o_ref[span, :] = (f_ref[span, :].astype(F32) + ADAPTER_SCALE * adapter).astype(BF16)

    return pl.pallas_call(
        kernel,
        out_shape=jax.ShapeDtypeStruct(frozen.shape, BF16),
        in_specs=[SMEM, VMEM, VMEM, VMEM],
        out_specs=VMEM,
        compiler_params=params(),
        cost_estimate=cost(2 * frozen.size * up.shape[1], 8 * frozen.size),
        name="finish_projected",
    )(holders, frozen, lowrank, up)


def input_product(holders, dy_full, value_matrix, back_low, down):
    rows, columns = dy_full.shape
    features = value_matrix.shape[0]
    rank = down.shape[1]
    group = 4

    def kernel(h_ref, dy_ref, v_ref, b_ref, down_ref, o_ref):
        first = pl.program_id(0) * group
        frozen = dot(dy_ref[...], v_ref[...], (1, 1))
        for tile in range(group):
            span = slice(tile * TILE, (tile + 1) * TILE)
            adapter = dot(b_ref[tile], down_ref[h_ref[first + tile]], (0, 0))
            o_ref[span, :] = (frozen[span, :] + ADAPTER_SCALE * adapter).astype(BF16)

    return pl.pallas_call(
        kernel,
        grid=(rows // (group * TILE),),
        out_shape=jax.ShapeDtypeStruct((rows, features), BF16),
        in_specs=[
            SMEM,
            pl.BlockSpec((group * TILE, columns), lambda i: (i, 0)),
            pl.BlockSpec(value_matrix.shape, lambda i: (0, 0)),
            pl.BlockSpec((group, rank, TILE), lambda i: (i, 0, 0)),
            pl.BlockSpec(down.shape, lambda i: (0, 0, 0)),
        ],
        out_specs=pl.BlockSpec((group * TILE, features), lambda i: (i, 0)),
        compiler_params=params(),
        cost_estimate=cost(2 * rows * columns * features, 2 * (dy_full.size + value_matrix.size + rows * features)),
        name="input_product",
    )(holders, dy_full, value_matrix, back_low, down)


def sum_over_tensor(part, half):
    size = lax.axis_size("tensor")
    chips = size // 2
    count = part.shape[0] // 2
    swap = [(i, i ^ 1) for i in range(size)]

    def along_x(array, k):
        return lax.ppermute(array, "tensor", [(i, (i // 2 + k) % chips * 2 + i % 2) for i in range(size)])

    both = (part.astype(F32) + lax.ppermute(part, "tensor", swap).astype(F32)).astype(BF16)
    own = lax.dynamic_slice_in_dim(both, half * count, count, 0)
    total = own.astype(F32)
    for k in range(1, chips):
        total = total + along_x(own, k).astype(F32)
    total = total.astype(BF16)
    other = lax.ppermute(total, "tensor", swap)
    first = jnp.where(half == 0, total, other)
    second = jnp.where(half == 0, other, total)
    return jnp.concatenate([first, second], axis=0)


def shards(
    tokens,
    cotangent,
    value_matrix,
    down_factors,
    up_factors,
    tile_usage_entry,
    usage,
    storage_row_map,
):
    owners = lax.axis_size("dp")
    tensor_size = lax.axis_size("tensor")
    half = lax.axis_index("tensor") % 2
    me = lax.axis_index("dp").astype(jnp.int32).reshape(1)
    holding = down_factors.shape[0]
    down_stored = jnp.transpose(down_factors, (0, 2, 1))

    dy_full = lax.all_gather(cotangent, "tensor", axis=1, tiled=True)
    rows, holders, send_up = route_up(me, usage, storage_row_map, tile_usage_entry, up_factors, holding)
    up = lax.all_to_all(send_up, "dp", split_axis=0, concat_axis=0, tiled=True)
    send_down = select_rows(rows, down_stored)
    down = lax.all_to_all(send_down, "dp", split_axis=0, concat_axis=0, tiled=True)

    base_part = base_product(tokens, value_matrix, tensor_size)
    frozen = lax.psum_scatter(base_part, "tensor", scatter_dimension=0, tiled=False)

    back_low = sum_over_tensor(back_product(holders, up, cotangent), half)
    send_down_terms = gradient_terms(holders, back_low, tokens, owners, 256)
    down_terms = lax.all_to_all(send_down_terms, "dp", split_axis=0, concat_axis=0, tiled=True)

    lowrank = sum_over_tensor(low_product(holders, down, tokens), half)
    send_up_terms = gradient_terms(holders, lowrank, cotangent, owners, cotangent.shape[1])
    up_terms = lax.all_to_all(send_up_terms, "dp", split_axis=0, concat_axis=0, tiled=True)

    input_gradient = input_product(holders, dy_full, value_matrix, back_low, down)
    projected = finish_projected(holders, frozen, lowrank, up)
    up_gradient = combine(rows, up_terms, holding, up_terms.shape[2])
    down_gradient = jnp.transpose(combine(rows, down_terms, holding, 256), (0, 2, 1))
    return (projected, input_gradient, down_gradient, up_gradient)


def solution(mesh):
    return jax.shard_map(
        shards,
        mesh=mesh,
        in_specs=(
            P("dp", "tensor"),
            P("dp", "tensor"),
            P("tensor", None),
            P("dp", "tensor", None),
            P("dp", None, "tensor"),
            P("dp"),
            P(),
            P(),
        ),
        out_specs=(
            P("dp", "tensor"),
            P("dp", "tensor"),
            P("dp", "tensor", None),
            P("dp", None, "tensor"),
        ),
        check_vma=False,
    )
```

```python
import jax
import jax.numpy as jnp
from jax import lax
from jax.experimental import pallas as pl
from jax.experimental.pallas import tpu as pltpu
from jax.sharding import PartitionSpec as P

TILE = 128
ADAPTER_SCALE = 2.0
F32 = jnp.float32
BF16 = jnp.bfloat16
HBM = pl.BlockSpec(memory_space=pltpu.HBM)
SMEM = pl.BlockSpec(memory_space=pltpu.SMEM)
VMEM = pl.BlockSpec(memory_space=pltpu.VMEM)
LIMIT = 62 * 1024 * 1024


def dot(a, b, contract):
    return lax.dot_general(a, b, ((contract[:1], contract[1:]), ((), ())), preferred_element_type=F32)


def cost(nbytes=1024):
    return pl.CostEstimate(flops=1024, bytes_accessed=nbytes, transcendentals=0)


def after(value, *others):
    return lax.optimization_barrier((value,) + others)[0]


def params():
    return pltpu.CompilerParams(vmem_limit_bytes=LIMIT)


def pass_on(copies, held, target, sems):
    count = len(copies)
    onward = []
    for index, copy in enumerate(copies):
        copy.wait()
        onward.append(pltpu.make_async_copy(held.at[index], target.at[index], sems.at[count + index]))
        onward[-1].start()
    for copy in onward:
        copy.wait()


def route_up(usage, storage_row_map, entries, up, holding):
    users = lax.axis_size("dp")
    tiles = entries.shape[0]
    slots = usage.shape[0] // users

    def kernel(usage_hbm, map_hbm, entry_hbm, up_ref, rows_ref, holders_ref, send_ref, usage_ref, map_ref, entry_ref, held, sems, table_sems):
        tables = [
            pltpu.make_async_copy(source, target, table_sems.at[index])
            for index, (source, target) in enumerate(
                ((usage_hbm, usage_ref), (map_hbm, map_ref), (entry_hbm, entry_ref))
            )
        ]
        for copy in tables:
            copy.start()
        for copy in tables:
            copy.wait()
        mine = lax.axis_index("dp").astype(jnp.int32)
        copies = []
        for user in range(users):
            row = jnp.int32(-1)
            for slot in range(slots):
                place = map_ref[usage_ref[user * slots + slot]]
                row = jnp.where(place // holding == mine, place % holding, row)
            rows_ref[user] = row
            copies.append(
                pltpu.make_async_copy(up_ref.at[jnp.maximum(row, 0)], held.at[user], sems.at[user])
            )
            copies[-1].start()
        for tile in range(tiles):
            holders_ref[tile] = map_ref[usage_ref[mine * slots + entry_ref[tile]]] // holding
        pass_on(copies, held, send_ref, sems)

    return pl.pallas_call(
        kernel,
        out_shape=(
            jax.ShapeDtypeStruct((users,), jnp.int32),
            jax.ShapeDtypeStruct((tiles,), jnp.int32),
            jax.ShapeDtypeStruct((users,) + up.shape[1:], BF16),
        ),
        in_specs=[HBM, HBM, HBM, HBM],
        out_specs=(SMEM, SMEM, HBM),
        scratch_shapes=[
            pltpu.SMEM(usage.shape, jnp.int32),
            pltpu.SMEM(storage_row_map.shape, jnp.int32),
            pltpu.SMEM(entries.shape, jnp.int32),
            pltpu.VMEM((users,) + up.shape[1:], BF16),
            pltpu.SemaphoreType.DMA((2 * users,)),
            pltpu.SemaphoreType.DMA((3,)),
        ],
        compiler_params=params(),
        cost_estimate=cost(),
        name="route_up",
    )(usage, storage_row_map, entries, up)


def select_rows(rows, stored):
    users = rows.shape[0]

    def kernel(rows_ref, stored_ref, send_ref, held, sems):
        copies = []
        for user in range(users):
            row = jnp.maximum(rows_ref[user], 0)
            copies.append(pltpu.make_async_copy(stored_ref.at[row], held.at[user], sems.at[user]))
            copies[-1].start()
        pass_on(copies, held, send_ref, sems)

    return pl.pallas_call(
        kernel,
        out_shape=jax.ShapeDtypeStruct((users,) + stored.shape[1:], BF16),
        in_specs=[SMEM, HBM],
        out_specs=HBM,
        scratch_shapes=[
            pltpu.VMEM((users,) + stored.shape[1:], BF16),
            pltpu.SemaphoreType.DMA((2 * users,)),
        ],
        compiler_params=params(),
        cost_estimate=cost(),
        name="select_down",
    )(rows, stored)


def base_product(tokens, value_matrix, shards_number):
    rows, features = tokens.shape
    columns = value_matrix.shape[1]
    width = columns // shards_number
    block = 512

    def kernel(x_ref, v_ref, o_ref):
        product = dot(x_ref[...], v_ref[...], (1, 0))
        for index in range(shards_number):
            o_ref[index] = product[:, index * width : (index + 1) * width].astype(BF16)

    return pl.pallas_call(
        kernel,
        grid=(rows // block,),
        out_shape=jax.ShapeDtypeStruct((shards_number, rows, width), BF16),
        in_specs=[
            pl.BlockSpec((block, features), lambda i: (i, 0)),
            pl.BlockSpec((features, columns), lambda i: (0, 0)),
        ],
        out_specs=pl.BlockSpec((shards_number, block, width), lambda i: (0, i, 0)),
        compiler_params=params(),
        cost_estimate=cost(),
        name="base_product",
    )(tokens, value_matrix)


def back_product(holders, up, cotangent):
    tiles = holders.shape[0]

    def kernel(h_ref, up_ref, dy_ref, o_ref):
        for tile in range(tiles):
            o_ref[tile] = dot(
                up_ref[h_ref[tile]], dy_ref[tile * TILE : (tile + 1) * TILE, :], (1, 1)
            ).astype(BF16)

    return pl.pallas_call(
        kernel,
        out_shape=jax.ShapeDtypeStruct((tiles, up.shape[1], TILE), BF16),
        in_specs=[SMEM, VMEM, VMEM],
        out_specs=VMEM,
        compiler_params=params(),
        cost_estimate=cost(),
        name="back_product",
    )(holders, up, cotangent)


def low_product(holders, down, tokens):
    tiles = holders.shape[0]
    rows, features = tokens.shape
    rank = down.shape[1]
    group = 4

    def kernel(h_ref, down_ref, x_ref, o_ref):
        first = pl.program_id(0) * group
        for tile in range(group):
            o_ref[tile] = dot(
                down_ref[h_ref[first + tile]], x_ref[tile * TILE : (tile + 1) * TILE, :], (1, 1)
            ).astype(BF16)

    return pl.pallas_call(
        kernel,
        grid=(tiles // group,),
        out_shape=jax.ShapeDtypeStruct((tiles, rank, TILE), BF16),
        in_specs=[
            SMEM,
            pl.BlockSpec(down.shape, lambda i: (0, 0, 0)),
            pl.BlockSpec((group * TILE, features), lambda i: (i, 0)),
        ],
        out_specs=pl.BlockSpec((group, rank, TILE), lambda i: (i, 0, 0)),
        compiler_params=params(),
        cost_estimate=cost(),
        name="low_product",
    )(holders, down, tokens)


def gradient_terms(holders, rank_side, wide_side, owners, step):
    tiles, rank, _ = rank_side.shape
    rows, width = wide_side.shape

    def kernel(h_ref, r_ref, w_ref, o_ref, total):
        total[...] = jnp.zeros_like(total)
        for tile in range(tiles):
            total[h_ref[tile]] += dot(r_ref[tile], w_ref[tile * TILE : (tile + 1) * TILE, :], (1, 0))
        o_ref[...] = (ADAPTER_SCALE * total[...]).astype(BF16)

    return pl.pallas_call(
        kernel,
        grid=(width // step,),
        out_shape=jax.ShapeDtypeStruct((owners, rank, width), BF16),
        in_specs=[
            SMEM,
            pl.BlockSpec(rank_side.shape, lambda i: (0, 0, 0)),
            pl.BlockSpec((rows, step), lambda i: (0, i)),
        ],
        out_specs=pl.BlockSpec((owners, rank, step), lambda i: (0, 0, i)),
        scratch_shapes=[pltpu.VMEM((owners, rank, step), F32)],
        compiler_params=params(),
        cost_estimate=cost(),
        name="gradient_terms",
    )(holders, rank_side, wide_side)


def combine(rows, received, holding, step, nbytes):
    users, rank, width = received.shape

    def kernel(rows_ref, r_ref, o_ref, total):
        total[...] = jnp.zeros_like(total)
        for user in range(users):

            @pl.when(rows_ref[user] >= 0)
            def _():
                total[jnp.maximum(rows_ref[user], 0)] += r_ref[user].astype(F32)

        o_ref[...] = total[...].astype(BF16)

    return pl.pallas_call(
        kernel,
        grid=(width // step,),
        out_shape=jax.ShapeDtypeStruct((holding, rank, width), BF16),
        in_specs=[SMEM, pl.BlockSpec((users, rank, step), lambda i: (0, 0, i))],
        out_specs=pl.BlockSpec((holding, rank, step), lambda i: (0, 0, i)),
        scratch_shapes=[pltpu.VMEM((holding, rank, step), F32)],
        compiler_params=params(),
        cost_estimate=cost(nbytes),
        name="combine",
    )(rows, received)


def finish_projected(holders, frozen, lowrank, up):
    tiles = holders.shape[0]

    def kernel(h_ref, f_ref, l_ref, up_ref, o_ref):
        for tile in range(tiles):
            span = slice(tile * TILE, (tile + 1) * TILE)
            adapter = dot(l_ref[tile], up_ref[h_ref[tile]], (0, 0))
            o_ref[span, :] = (f_ref[span, :].astype(F32) + ADAPTER_SCALE * adapter).astype(BF16)

    return pl.pallas_call(
        kernel,
        out_shape=jax.ShapeDtypeStruct(frozen.shape, BF16),
        in_specs=[SMEM, VMEM, VMEM, VMEM],
        out_specs=VMEM,
        compiler_params=params(),
        cost_estimate=cost(),
        name="finish_projected",
    )(holders, frozen, lowrank, up)


def input_product(holders, dy_full, value_matrix, back_low, down):
    rows, columns = dy_full.shape
    features = value_matrix.shape[0]
    rank = down.shape[1]
    group = 4

    def kernel(h_ref, dy_ref, v_ref, b_ref, down_ref, o_ref):
        first = pl.program_id(0) * group
        frozen = dot(dy_ref[...], v_ref[...], (1, 1))
        for tile in range(group):
            span = slice(tile * TILE, (tile + 1) * TILE)
            adapter = dot(b_ref[tile], down_ref[h_ref[first + tile]], (0, 0))
            o_ref[span, :] = (frozen[span, :] + ADAPTER_SCALE * adapter).astype(BF16)

    return pl.pallas_call(
        kernel,
        grid=(rows // (group * TILE),),
        out_shape=jax.ShapeDtypeStruct((rows, features), BF16),
        in_specs=[
            SMEM,
            pl.BlockSpec((group * TILE, columns), lambda i: (i, 0)),
            pl.BlockSpec(value_matrix.shape, lambda i: (0, 0)),
            pl.BlockSpec((group, rank, TILE), lambda i: (i, 0, 0)),
            pl.BlockSpec(down.shape, lambda i: (0, 0, 0)),
        ],
        out_specs=pl.BlockSpec((group * TILE, features), lambda i: (i, 0)),
        compiler_params=params(),
        cost_estimate=cost(),
        name="input_product",
    )(holders, dy_full, value_matrix, back_low, down)


def swap_cores(array):
    size = lax.axis_size("tensor")
    return lax.ppermute(array, "tensor", [(i, i ^ 1) for i in range(size)])


def along_x(array, k):
    size = lax.axis_size("tensor")
    chips = size // 2
    return lax.ppermute(array, "tensor", [(i, (i // 2 + k) % chips * 2 + i % 2) for i in range(size)])


def sum_on_chip(part):
    return (part.astype(F32) + swap_cores(part).astype(F32)).astype(BF16)


def other_chips(own):
    return [along_x(own, k) for k in (1, -1, 2)]


def sum_of(own, others):
    total = own.astype(F32)
    for other in others:
        total = total + other.astype(F32)
    return total.astype(BF16)


def shards(
    tokens,
    cotangent,
    value_matrix,
    down_factors,
    up_factors,
    tile_usage_entry,
    usage,
    storage_row_map,
):
    owners = lax.axis_size("dp")
    tensor_size = lax.axis_size("tensor")
    holding = down_factors.shape[0]
    down_stored = jnp.transpose(down_factors, (0, 2, 1))

    dy_full = lax.all_gather(cotangent, "tensor", axis=1, tiled=True)
    rows, holders, send_up = route_up(usage, storage_row_map, tile_usage_entry, up_factors, holding)
    up = lax.all_to_all(send_up, "dp", split_axis=0, concat_axis=0, tiled=True)
    send_down = select_rows(rows, down_stored)
    down = lax.all_to_all(send_down, "dp", split_axis=0, concat_axis=0, tiled=True)

    base_part = base_product(after(tokens, rows), value_matrix, tensor_size)
    frozen = lax.psum_scatter(base_part, "tensor", scatter_dimension=0, tiled=False)
    back_part = back_product(holders, after(up, send_down, base_part), cotangent)
    back_chip = sum_on_chip(back_part)
    back_low = sum_of(back_chip, other_chips(back_chip))
    send_down_terms = gradient_terms(holders, back_low, tokens, owners, 256)
    down_terms = lax.all_to_all(send_down_terms, "dp", split_axis=0, concat_axis=0, tiled=True)

    low_chip = sum_on_chip(low_product(holders, after(down, send_down_terms), tokens))
    low_others = other_chips(low_chip)
    input_gradient = input_product(holders, after(dy_full, low_chip), value_matrix, back_low, down)
    low_others[2] = after(low_others[2], input_gradient)
    lowrank = sum_of(low_chip, low_others)
    send_up_terms = gradient_terms(holders, lowrank, cotangent, owners, cotangent.shape[1])
    down_terms, send_up_terms = lax.optimization_barrier((down_terms, send_up_terms))
    up_terms = lax.all_to_all(send_up_terms, "dp", split_axis=0, concat_axis=0, tiled=True)

    projected = finish_projected(holders, frozen, lowrank, up)
    up_gradient = combine(rows, after(up_terms, projected), holding, up_terms.shape[2], 1024)
    down_gradient = jnp.transpose(combine(rows, down_terms, holding, 256, 1 << 30), (0, 2, 1))
    return (projected, input_gradient, down_gradient, up_gradient)


def solution(mesh):
    return jax.shard_map(
        shards,
        mesh=mesh,
        in_specs=(
            P("dp", "tensor"),
            P("dp", "tensor"),
            P("tensor", None),
            P("dp", "tensor", None),
            P("dp", None, "tensor"),
            P("dp"),
            P(),
            P(),
        ),
        out_specs=(
            P("dp", "tensor"),
            P("dp", "tensor"),
            P("dp", "tensor", None),
            P("dp", None, "tensor"),
        ),
        check_vma=False,
    )
```

```python
import jax
import jax.numpy as jnp
from jax import lax
from jax.experimental import pallas as pl
from jax.experimental.pallas import tpu as pltpu
from jax.sharding import PartitionSpec as P

TILE = 128
ADAPTER_SCALE = 2.0
F32 = jnp.float32
BF16 = jnp.bfloat16
HBM = pl.BlockSpec(memory_space=pltpu.HBM)
ANY = pl.BlockSpec(memory_space=pl.ANY)
SMEM = pl.BlockSpec(memory_space=pltpu.SMEM)
VMEM = pl.BlockSpec(memory_space=pltpu.VMEM)
SHIFTS = (0, 1, -1, 2)
LIMIT = 62 * 1024 * 1024
PART = 24 * 1024 * 1024


def dot(a, b, contract):
    return lax.dot_general(a, b, ((contract[:1], contract[1:]), ((), ())), preferred_element_type=F32)


def cost(flops=1024):
    return pl.CostEstimate(flops=flops, bytes_accessed=1024, transcendentals=0)


def after(value, *others):
    return lax.optimization_barrier((value,) + others)[0]


def params(limit=LIMIT):
    return pltpu.CompilerParams(vmem_limit_bytes=limit)


def pass_on(copies, held, target, sems):
    count = len(copies)
    onward = []
    for index, copy in enumerate(copies):
        copy.wait()
        onward.append(pltpu.make_async_copy(held.at[index], target.at[index], sems.at[count + index]))
        onward[-1].start()
    for copy in onward:
        copy.wait()


def route_up(usage, storage_row_map, entries, up, holding):
    users = lax.axis_size("dp")
    tiles = entries.shape[0]
    slots = usage.shape[0] // users

    def kernel(usage_hbm, map_hbm, entry_hbm, up_ref, rows_ref, holders_ref, send_ref, usage_ref, map_ref, entry_ref, held, sems, table_sems):
        tables = [
            pltpu.make_async_copy(source, target, table_sems.at[index])
            for index, (source, target) in enumerate(
                ((usage_hbm, usage_ref), (map_hbm, map_ref), (entry_hbm, entry_ref))
            )
        ]
        for copy in tables:
            copy.start()
        for copy in tables:
            copy.wait()
        mine = lax.axis_index("dp").astype(jnp.int32)
        copies = []
        for user in range(users):
            row = jnp.int32(-1)
            for slot in range(slots):
                place = map_ref[usage_ref[user * slots + slot]]
                row = jnp.where(place // holding == mine, place % holding, row)
            rows_ref[user] = row
            copies.append(
                pltpu.make_async_copy(up_ref.at[jnp.maximum(row, 0)], held.at[user], sems.at[user])
            )
            copies[-1].start()
        for tile in range(tiles):
            holders_ref[tile] = map_ref[usage_ref[mine * slots + entry_ref[tile]]] // holding
        pass_on(copies, held, send_ref, sems)

    return pl.pallas_call(
        kernel,
        out_shape=(
            jax.ShapeDtypeStruct((users,), jnp.int32),
            jax.ShapeDtypeStruct((tiles,), jnp.int32),
            jax.ShapeDtypeStruct((users,) + up.shape[1:], BF16),
        ),
        in_specs=[HBM, HBM, HBM, HBM],
        out_specs=(SMEM, SMEM, HBM),
        scratch_shapes=[
            pltpu.SMEM(usage.shape, jnp.int32),
            pltpu.SMEM(storage_row_map.shape, jnp.int32),
            pltpu.SMEM(entries.shape, jnp.int32),
            pltpu.VMEM((users,) + up.shape[1:], BF16),
            pltpu.SemaphoreType.DMA((2 * users,)),
            pltpu.SemaphoreType.DMA((3,)),
        ],
        compiler_params=params(),
        cost_estimate=cost(),
        name="route_up",
    )(usage, storage_row_map, entries, up)


def select_rows(rows, stored):
    users = rows.shape[0]

    def kernel(rows_ref, stored_ref, send_ref, held, sems):
        copies = []
        for user in range(users):
            row = jnp.maximum(rows_ref[user], 0)
            copies.append(pltpu.make_async_copy(stored_ref.at[row], held.at[user], sems.at[user]))
            copies[-1].start()
        pass_on(copies, held, send_ref, sems)

    return pl.pallas_call(
        kernel,
        out_shape=jax.ShapeDtypeStruct((users,) + stored.shape[1:], BF16),
        in_specs=[SMEM, HBM],
        out_specs=HBM,
        scratch_shapes=[
            pltpu.VMEM((users,) + stored.shape[1:], BF16),
            pltpu.SemaphoreType.DMA((2 * users,)),
        ],
        compiler_params=params(),
        cost_estimate=cost(),
        name="select_down",
    )(rows, stored)


def relative_columns(flip):
    size = lax.axis_size("tensor")
    me = lax.axis_index("tensor").astype(jnp.int32)
    chips = size // 2
    core = me % 2 if flip == 0 else 1 - me % 2
    return [(me // 2 + chips + shift) % chips * 2 + core for shift in SHIFTS]


def start_all(copies):
    for copy in copies:
        copy.start()
    return copies


def wait_all(copies):
    for copy in copies:
        copy.wait()


def base_product(tokens, value_matrix):
    rows, features = tokens.shape
    columns = value_matrix.shape[1]
    width = columns // lax.axis_size("tensor")
    chips = len(SHIFTS)
    steps = 4
    block = rows // steps

    def kernel(x_hbm, v_hbm, own_hbm, other_hbm, x_ref, v_ref, y_ref, in_sems, out_sems):
        core = lax.axis_index("tensor").astype(jnp.int32) % 2
        spans = [pl.ds(step * block, block) for step in range(steps)]
        fetch = start_all(
            [pltpu.make_async_copy(v_hbm, v_ref, in_sems.at[steps])]
            + [
                pltpu.make_async_copy(x_hbm.at[span], x_ref.at[span], in_sems.at[step])
                for step, span in enumerate(spans)
            ]
        )
        fetch[0].wait()
        stores = []
        for step, span in enumerate(spans):
            fetch[1 + step].wait()
            product = dot(x_ref[span, :], v_ref[...], (1, 0)).astype(BF16)
            for index in range(2 * chips):
                y_ref[index % 2, index // 2, span, :] = product[:, index * width : (index + 1) * width]
            stores += start_all(
                [
                    pltpu.make_async_copy(y_ref.at[core, :, span], own_hbm.at[:, span], out_sems.at[0, step]),
                    pltpu.make_async_copy(y_ref.at[1 - core, :, span], other_hbm.at[:, span], out_sems.at[1, step]),
                ]
            )
        wait_all(stores)

    shape = jax.ShapeDtypeStruct((chips, rows, width), BF16)
    return pl.pallas_call(
        kernel,
        out_shape=(shape, shape),
        in_specs=[HBM, HBM],
        out_specs=(HBM, HBM),
        scratch_shapes=[
            pltpu.VMEM(tokens.shape, BF16),
            pltpu.VMEM(value_matrix.shape, BF16),
            pltpu.VMEM((2, chips, rows, width), BF16),
            pltpu.SemaphoreType.DMA((steps + 1,)),
            pltpu.SemaphoreType.DMA((2, steps)),
        ],
        compiler_params=params(PART),
        cost_estimate=cost(),
        name="base_product",
    )(tokens, value_matrix)


def add_cores(own, other):
    chips, rows, width = own.shape

    def kernel(own_hbm, other_hbm, *refs):
        sums = refs[:chips]
        own_ref, other_ref, sum_ref, in_sems, out_sems = refs[chips:]
        mine = lax.axis_index("tensor").astype(jnp.int32) // 2
        fetch = []
        for index, shift in enumerate(SHIFTS):
            chip = (mine + chips + shift) % chips
            fetch += start_all(
                [
                    pltpu.make_async_copy(own_hbm.at[chip], own_ref.at[index], in_sems.at[0, index]),
                    pltpu.make_async_copy(other_hbm.at[chip], other_ref.at[index], in_sems.at[1, index]),
                ]
            )
        stores = []
        for index in range(chips):
            wait_all(fetch[2 * index : 2 * index + 2])
            sum_ref[index] = (own_ref[index].astype(F32) + other_ref[index].astype(F32)).astype(BF16)
            stores += start_all([pltpu.make_async_copy(sum_ref.at[index], sums[index], out_sems.at[index])])
        wait_all(stores)

    return pl.pallas_call(
        kernel,
        out_shape=[jax.ShapeDtypeStruct((rows, width), BF16)] * chips,
        in_specs=[ANY, ANY],
        out_specs=[ANY] * chips,
        scratch_shapes=[pltpu.VMEM(own.shape, BF16)] * 3
        + [pltpu.SemaphoreType.DMA((2, chips)), pltpu.SemaphoreType.DMA((chips,))],
        compiler_params=params(PART),
        cost_estimate=cost(),
        name="add_cores",
    )(own, other)


def back_product(holders, up, cotangent):
    tiles = holders.shape[0]

    def kernel(h_ref, up_ref, dy_ref, o_ref):
        for tile in range(tiles):
            o_ref[tile] = dot(
                up_ref[h_ref[tile]], dy_ref[tile * TILE : (tile + 1) * TILE, :], (1, 1)
            ).astype(BF16)

    return pl.pallas_call(
        kernel,
        out_shape=jax.ShapeDtypeStruct((tiles, up.shape[1], TILE), BF16),
        in_specs=[SMEM, VMEM, VMEM],
        out_specs=VMEM,
        compiler_params=params(PART),
        cost_estimate=cost(),
        name="back_product",
    )(holders, up, cotangent)


def low_product(holders, down, tokens):
    tiles = holders.shape[0]
    rows, features = tokens.shape
    rank = down.shape[1]
    steps = 4
    block = rows // steps

    def kernel(h_ref, down_hbm, x_hbm, o_ref, down_ref, x_ref, sems):
        fetch = start_all(
            [pltpu.make_async_copy(down_hbm, down_ref, sems.at[steps])]
            + [
                pltpu.make_async_copy(x_hbm.at[span], x_ref.at[span], sems.at[step])
                for step, span in enumerate([pl.ds(step * block, block) for step in range(steps)])
            ]
        )
        fetch[0].wait()
        for tile in range(tiles):
            if tile * TILE % block == 0:
                fetch[1 + tile * TILE // block].wait()
            o_ref[tile] = dot(
                down_ref[h_ref[tile]], x_ref[tile * TILE : (tile + 1) * TILE, :], (1, 1)
            ).astype(BF16)

    return pl.pallas_call(
        kernel,
        out_shape=jax.ShapeDtypeStruct((tiles, rank, TILE), BF16),
        in_specs=[SMEM, ANY, ANY],
        out_specs=VMEM,
        scratch_shapes=[
            pltpu.VMEM(down.shape, BF16),
            pltpu.VMEM(tokens.shape, BF16),
            pltpu.SemaphoreType.DMA((steps + 1,)),
        ],
        compiler_params=params(PART),
        cost_estimate=cost(1 << 40),
        name="low_product",
    )(holders, down, tokens)


def narrow_terms(holders, rank_side, wide_side, owners):
    tiles, rank, _ = rank_side.shape
    width = wide_side.shape[1]

    def kernel(h_ref, r_ref, w_ref, o_ref, total):
        total[...] = jnp.zeros_like(total)
        for tile in range(tiles):
            total[h_ref[tile]] += dot(r_ref[tile], w_ref[tile * TILE : (tile + 1) * TILE, :], (1, 0))
        o_ref[...] = (ADAPTER_SCALE * total[...]).astype(BF16)

    return pl.pallas_call(
        kernel,
        out_shape=jax.ShapeDtypeStruct((owners, rank, width), BF16),
        in_specs=[SMEM, VMEM, VMEM],
        out_specs=VMEM,
        scratch_shapes=[pltpu.VMEM((owners, rank, width), F32)],
        compiler_params=params(PART),
        cost_estimate=cost(),
        name="narrow_terms",
    )(holders, rank_side, wide_side)


def narrow_combine(rows, received, holding):
    users, rank, width = received.shape

    def kernel(rows_ref, r_ref, o_ref, total):
        total[...] = jnp.zeros_like(total)
        for user in range(users):

            @pl.when(rows_ref[user] >= 0)
            def _():
                total[jnp.maximum(rows_ref[user], 0)] += r_ref[user].astype(F32)

        o_ref[...] = total[...].astype(BF16)

    return pl.pallas_call(
        kernel,
        out_shape=jax.ShapeDtypeStruct((holding, rank, width), BF16),
        in_specs=[SMEM, VMEM],
        out_specs=VMEM,
        scratch_shapes=[pltpu.VMEM((holding, rank, width), F32)],
        compiler_params=params(PART),
        cost_estimate=cost(),
        name="narrow_combine",
    )(rows, received)


def gradient_terms(holders, rank_side, wide_side, owners):
    tiles, rank, _ = rank_side.shape
    rows, width = wide_side.shape
    steps = 4
    block = rows // steps

    def kernel(h_ref, r_hbm, w_hbm, o_hbm, r_ref, w_ref, total, o_ref, in_sems, out_sems):
        fetch = start_all(
            [pltpu.make_async_copy(r_hbm, r_ref, in_sems.at[steps])]
            + [
                pltpu.make_async_copy(w_hbm.at[span], w_ref.at[span], in_sems.at[step])
                for step, span in enumerate([pl.ds(step * block, block) for step in range(steps)])
            ]
        )
        total[...] = jnp.zeros_like(total)
        fetch[0].wait()
        for tile in range(tiles):
            if tile * TILE % block == 0:
                fetch[1 + tile * TILE // block].wait()
            total[h_ref[tile]] += dot(r_ref[tile], w_ref[tile * TILE : (tile + 1) * TILE, :], (1, 0))
        stores = []
        part = owners // 4
        for index in range(4):
            span = pl.ds(index * part, part)
            o_ref[span] = (ADAPTER_SCALE * total[span]).astype(BF16)
            stores += start_all([pltpu.make_async_copy(o_ref.at[span], o_hbm.at[span], out_sems.at[index])])
        wait_all(stores)

    return pl.pallas_call(
        kernel,
        out_shape=jax.ShapeDtypeStruct((owners, rank, width), BF16),
        in_specs=[SMEM, ANY, ANY],
        out_specs=HBM,
        scratch_shapes=[
            pltpu.VMEM(rank_side.shape, BF16),
            pltpu.VMEM(wide_side.shape, BF16),
            pltpu.VMEM((owners, rank, width), F32),
            pltpu.VMEM((owners, rank, width), BF16),
            pltpu.SemaphoreType.DMA((steps + 1,)),
            pltpu.SemaphoreType.DMA((4,)),
        ],
        compiler_params=params(PART),
        cost_estimate=cost(),
        name="gradient_terms",
    )(holders, rank_side, wide_side)


def combine(rows, received, holding):
    users, rank, width = received.shape
    steps = 4
    part = rank // steps

    def kernel(rows_ref, r_hbm, o_hbm, r_ref, total, o_ref, in_sems, out_sems):
        spans = [pl.ds(step * part, part) for step in range(steps)]
        fetch = start_all(
            [
                pltpu.make_async_copy(r_hbm.at[:, span], r_ref.at[:, span], in_sems.at[step])
                for step, span in enumerate(spans)
            ]
        )
        stores = []
        for step, span in enumerate(spans):
            total[...] = jnp.zeros_like(total)
            fetch[step].wait()
            for user in range(users):

                @pl.when(rows_ref[user] >= 0)
                def _():
                    total[jnp.maximum(rows_ref[user], 0)] += r_ref[user, span].astype(F32)

            o_ref[:, span] = total[...].astype(BF16)
            stores += start_all([pltpu.make_async_copy(o_ref.at[:, span], o_hbm.at[:, span], out_sems.at[step])])
        wait_all(stores)

    return pl.pallas_call(
        kernel,
        out_shape=jax.ShapeDtypeStruct((holding, rank, width), BF16),
        in_specs=[SMEM, ANY],
        out_specs=HBM,
        scratch_shapes=[
            pltpu.VMEM(received.shape, BF16),
            pltpu.VMEM((holding, part, width), F32),
            pltpu.VMEM((holding, rank, width), BF16),
            pltpu.SemaphoreType.DMA((steps,)),
            pltpu.SemaphoreType.DMA((steps,)),
        ],
        compiler_params=params(PART),
        cost_estimate=cost(),
        name="combine",
    )(rows, received)


def finish_projected(holders, terms, lowrank, up):
    tiles = holders.shape[0]
    rows, width = terms[0].shape
    count = len(terms)
    middle = rows // 2

    def kernel(h_ref, *refs):
        l_hbm, up_hbm, o_hbm, t_ref, l_ref, up_ref, o_ref, term_sems, in_sems, out_sems = refs[count:]
        spans = [pl.ds(half * middle, middle) for half in range(2)]
        fetch = start_all(
            [
                pltpu.make_async_copy(source, target, in_sems.at[index])
                for index, (source, target) in enumerate(((l_hbm, l_ref), (up_hbm, up_ref)))
            ]
        )
        halves = [
            start_all(
                [
                    pltpu.make_async_copy(
                        refs[index].at[span], t_ref.at[index, span], term_sems.at[half, index]
                    )
                    for index in range(count)
                ]
            )
            for half, span in enumerate(spans)
        ]
        wait_all(fetch)
        stores = []
        for half, span in enumerate(spans):
            wait_all(halves[half])
            for tile in range(half * tiles // 2, (half + 1) * tiles // 2):
                rows_of = pl.ds(tile * TILE, TILE)
                total = ADAPTER_SCALE * dot(l_ref[tile], up_ref[h_ref[tile]], (0, 0))
                for index in range(count):
                    total = total + t_ref[index, rows_of, :].astype(F32)
                o_ref[rows_of, :] = total.astype(BF16)
            stores += start_all([pltpu.make_async_copy(o_ref.at[span], o_hbm.at[span], out_sems.at[half])])
        wait_all(stores)

    return pl.pallas_call(
        kernel,
        out_shape=jax.ShapeDtypeStruct((rows, width), BF16),
        in_specs=[SMEM] + [ANY] * (count + 2),
        out_specs=HBM,
        scratch_shapes=[
            pltpu.VMEM((count, rows, width), BF16),
            pltpu.VMEM(lowrank.shape, BF16),
            pltpu.VMEM(up.shape, BF16),
            pltpu.VMEM((rows, width), BF16),
            pltpu.SemaphoreType.DMA((2, count)),
            pltpu.SemaphoreType.DMA((2,)),
            pltpu.SemaphoreType.DMA((2,)),
        ],
        compiler_params=params(PART),
        cost_estimate=cost(),
        name="finish_projected",
    )(holders, *terms, lowrank, up)


def input_product(holders, pieces, value_matrix, back_low, down):
    rows, width = pieces[0].shape
    features, columns = value_matrix.shape
    steps = 4
    block = rows // steps
    group = block // TILE
    middle = rows // 2
    count = len(pieces)

    def kernel(h_ref, *refs):
        hbm = refs[:count]
        v_hbm, b_hbm, down_hbm, o_hbm = refs[count : count + 4]
        dy_ref, v_ref, b_ref, down_ref, o_ref, dy_sems, in_sems, out_sems = refs[count + 4 :]
        halves = []
        for half in range(2):
            span = pl.ds(half * middle, middle)
            copies = []
            for flip in range(2):
                own, after_own, before_own, opposite = relative_columns(flip)
                own_hbm, left_hbm, right_hbm, first_hbm, last_hbm = hbm[flip * count // 2 : (flip + 1) * count // 2]
                sources = (
                    (own, own_hbm.at[span]),
                    (before_own, left_hbm.at[span]),
                    (after_own, right_hbm.at[span]),
                    (opposite, (first_hbm, last_hbm)[half]),
                )
                for index, (place, source) in enumerate(sources):
                    target = dy_ref.at[span, pl.ds(pl.multiple_of(place * width, width), width)]
                    copies.append(pltpu.make_async_copy(source, target, dy_sems.at[half, flip, index]))
            halves.append(copies)
        fetch = [
            pltpu.make_async_copy(source, target, in_sems.at[index])
            for index, (source, target) in enumerate(((v_hbm, v_ref), (b_hbm, b_ref), (down_hbm, down_ref)))
        ]
        first = start_all(fetch[:1] + halves[0])
        stores = []
        for step in range(steps):
            if step == 0:
                wait_all(first)
                start_all(fetch[1:])
            elif step * block == middle:
                wait_all(halves[1])
            span = pl.ds(step * block, block)
            frozen = dot(dy_ref[span, :], v_ref[...], (1, 1))
            if step == 0:
                wait_all(fetch[1:])
                start_all(halves[1])
            for tile in range(group):
                adapter = dot(b_ref[step * group + tile], down_ref[h_ref[step * group + tile]], (0, 0))
                o_ref[pl.ds(step * block + tile * TILE, TILE), :] = (
                    frozen[tile * TILE : (tile + 1) * TILE, :] + ADAPTER_SCALE * adapter
                ).astype(BF16)
            stores += start_all([pltpu.make_async_copy(o_ref.at[span], o_hbm.at[span], out_sems.at[step])])
        wait_all(stores)

    return pl.pallas_call(
        kernel,
        out_shape=jax.ShapeDtypeStruct((rows, features), BF16),
        in_specs=[SMEM] + [ANY] * (count + 3),
        out_specs=HBM,
        scratch_shapes=[
            pltpu.VMEM((rows, columns), BF16),
            pltpu.VMEM(value_matrix.shape, BF16),
            pltpu.VMEM(back_low.shape, BF16),
            pltpu.VMEM(down.shape, BF16),
            pltpu.VMEM((rows, features), BF16),
            pltpu.SemaphoreType.DMA((2, 2, 4)),
            pltpu.SemaphoreType.DMA((3,)),
            pltpu.SemaphoreType.DMA((steps,)),
        ],
        compiler_params=params(PART),
        cost_estimate=cost(),
        name="input_product",
    )(holders, *pieces, value_matrix, back_low, down)


def swap_cores(array):
    size = lax.axis_size("tensor")
    return lax.ppermute(array, "tensor", [(i, i ^ 1) for i in range(size)])


def along_x(array, k):
    size = lax.axis_size("tensor")
    chips = size // 2
    return lax.ppermute(array, "tensor", [(i, (i // 2 + k) % chips * 2 + i % 2) for i in range(size)])


def sum_on_chip(part):
    return (part.astype(F32) + swap_cores(part).astype(F32)).astype(BF16)


def other_chips(own):
    return [along_x(own, shift) for shift in SHIFTS[1:]]


def sum_of(own, others):
    total = own.astype(F32)
    for other in others:
        total = total + other.astype(F32)
    return total.astype(BF16)


def shards(
    tokens,
    cotangent,
    value_matrix,
    down_factors,
    up_factors,
    tile_usage_entry,
    usage,
    storage_row_map,
):
    owners = lax.axis_size("dp")
    holding = down_factors.shape[0]
    down_stored = jnp.transpose(down_factors, (0, 2, 1))

    middle = cotangent.shape[0] // 2
    rows, holders, send_up = route_up(usage, storage_row_map, tile_usage_entry, up_factors, holding)
    up = lax.all_to_all(send_up, "dp", split_axis=0, concat_axis=0, tiled=True)
    left, right = along_x(cotangent, 1), along_x(cotangent, -1)
    send_down = after(select_rows(rows, down_stored), left, right)
    down = lax.all_to_all(send_down, "dp", split_axis=0, concat_axis=0, tiled=True)

    first, last = along_x(left[:middle], 1), along_x(right[middle:], -1)
    own_swapped = swap_cores(cotangent)
    back_part = back_product(holders, after(up, send_down, own_swapped), cotangent)
    left_swapped, right_swapped = swap_cores(left), swap_cores(right)
    back_chip = after(sum_on_chip(back_part), left_swapped, right_swapped)
    back_others = other_chips(back_chip)
    own_base, other_base = base_product(after(tokens, back_chip), value_matrix)
    first_swapped, last_swapped = swap_cores(first), swap_cores(last)
    back_others[2] = after(back_others[2], own_base, first, last)
    back_low = sum_of(back_chip, back_others)
    pieces = [cotangent, left, right, first, last]
    pieces += [own_swapped, left_swapped, right_swapped, first_swapped, last_swapped]
    sums = add_cores(own_base, swap_cores(other_base))
    frozen = [sums[0]] + [along_x(part, shift) for part, shift in zip(sums[1:], SHIFTS[1:])]
    send_down_terms = gradient_terms(holders, back_low, tokens, owners)
    down_terms = lax.all_to_all(send_down_terms, "dp", split_axis=0, concat_axis=0, tiled=True)

    low_chip = sum_on_chip(low_product(holders, after(down, send_down_terms), tokens))
    low_others = other_chips(low_chip)
    pieces[0] = after(pieces[0], low_chip)
    input_gradient = input_product(holders, pieces, value_matrix, back_low, down)
    low_others[2] = after(low_others[2], input_gradient)
    lowrank = sum_of(low_chip, low_others)
    send_up_terms = narrow_terms(holders, lowrank, cotangent, owners)
    down_terms, send_up_terms = lax.optimization_barrier((down_terms, send_up_terms))
    up_terms = lax.all_to_all(send_up_terms, "dp", split_axis=0, concat_axis=0, tiled=True)

    projected = finish_projected(holders, frozen, lowrank, up)
    up_gradient = narrow_combine(rows, after(up_terms, projected), holding)
    down_gradient = jnp.transpose(combine(rows, down_terms, holding), (0, 2, 1))
    return (projected, input_gradient, down_gradient, up_gradient)


def solution(mesh):
    return jax.shard_map(
        shards,
        mesh=mesh,
        in_specs=(
            P("dp", "tensor"),
            P("dp", "tensor"),
            P("tensor", None),
            P("dp", "tensor", None),
            P("dp", None, "tensor"),
            P("dp"),
            P(),
            P(),
        ),
        out_specs=(
            P("dp", "tensor"),
            P("dp", "tensor"),
            P("dp", "tensor", None),
            P("dp", None, "tensor"),
        ),
        check_vma=False,
    )
```

```python
import jax
import jax.numpy as jnp
from jax import lax
from jax.experimental import pallas as pl
from jax.experimental.pallas import tpu as pltpu
from jax.sharding import PartitionSpec as P

TILE = 128
ADAPTER_SCALE = 2.0
F32 = jnp.float32
BF16 = jnp.bfloat16
HBM = pl.BlockSpec(memory_space=pltpu.HBM)
ANY = pl.BlockSpec(memory_space=pl.ANY)
SMEM = pl.BlockSpec(memory_space=pltpu.SMEM)
VMEM = pl.BlockSpec(memory_space=pltpu.VMEM)
SHIFTS = (0, 1, -1, 2)
LIMIT = 62 * 1024 * 1024
PART = 24 * 1024 * 1024


def dot(a, b, contract):
    return lax.dot_general(a, b, ((contract[:1], contract[1:]), ((), ())), preferred_element_type=F32)


def cost(flops=1024):
    return pl.CostEstimate(flops=flops, bytes_accessed=1024, transcendentals=0)


def in_hbm(value):
    return pltpu.with_memory_space_constraint(value, pltpu.HBM)


def after(value, *others):
    return lax.optimization_barrier((value,) + others)[0]


def params(limit=LIMIT):
    return pltpu.CompilerParams(vmem_limit_bytes=limit)


def pass_on(copies, held, target, sems):
    count = len(copies)
    onward = []
    for index, copy in enumerate(copies):
        copy.wait()
        onward.append(pltpu.make_async_copy(held.at[index], target.at[index], sems.at[count + index]))
        onward[-1].start()
    for copy in onward:
        copy.wait()


def route_up(usage, storage_row_map, entries, up, holding):
    users = lax.axis_size("dp")
    tiles = entries.shape[0]
    slots = usage.shape[0] // users

    def kernel(usage_hbm, map_hbm, entry_hbm, up_ref, rows_ref, holders_ref, send_ref, usage_ref, map_ref, entry_ref, held, sems, table_sems):
        tables = [
            pltpu.make_async_copy(source, target, table_sems.at[index])
            for index, (source, target) in enumerate(
                ((usage_hbm, usage_ref), (map_hbm, map_ref), (entry_hbm, entry_ref))
            )
        ]
        for copy in tables:
            copy.start()
        for copy in tables:
            copy.wait()
        mine = lax.axis_index("dp").astype(jnp.int32)
        copies = []
        for user in range(users):
            row = jnp.int32(-1)
            for slot in range(slots):
                place = map_ref[usage_ref[user * slots + slot]]
                row = jnp.where(place // holding == mine, place % holding, row)
            rows_ref[user] = row
            copies.append(
                pltpu.make_async_copy(up_ref.at[jnp.maximum(row, 0)], held.at[user], sems.at[user])
            )
            copies[-1].start()
        for tile in range(tiles):
            holders_ref[tile] = map_ref[usage_ref[mine * slots + entry_ref[tile]]] // holding
        pass_on(copies, held, send_ref, sems)

    return pl.pallas_call(
        kernel,
        out_shape=(
            jax.ShapeDtypeStruct((users,), jnp.int32),
            jax.ShapeDtypeStruct((tiles,), jnp.int32),
            jax.ShapeDtypeStruct((users,) + up.shape[1:], BF16),
        ),
        in_specs=[HBM, HBM, HBM, HBM],
        out_specs=(SMEM, SMEM, HBM),
        scratch_shapes=[
            pltpu.SMEM(usage.shape, jnp.int32),
            pltpu.SMEM(storage_row_map.shape, jnp.int32),
            pltpu.SMEM(entries.shape, jnp.int32),
            pltpu.VMEM((users,) + up.shape[1:], BF16),
            pltpu.SemaphoreType.DMA((2 * users,)),
            pltpu.SemaphoreType.DMA((3,)),
        ],
        compiler_params=params(),
        cost_estimate=cost(),
        name="route_up",
    )(usage, storage_row_map, entries, up)


def select_rows(rows, stored):
    users = rows.shape[0]

    def kernel(rows_ref, stored_ref, send_ref, held, sems):
        copies = []
        for user in range(users):
            row = jnp.maximum(rows_ref[user], 0)
            copies.append(pltpu.make_async_copy(stored_ref.at[row], held.at[user], sems.at[user]))
            copies[-1].start()
        pass_on(copies, held, send_ref, sems)

    return pl.pallas_call(
        kernel,
        out_shape=jax.ShapeDtypeStruct((users,) + stored.shape[1:], BF16),
        in_specs=[SMEM, HBM],
        out_specs=HBM,
        scratch_shapes=[
            pltpu.VMEM((users,) + stored.shape[1:], BF16),
            pltpu.SemaphoreType.DMA((2 * users,)),
        ],
        compiler_params=params(),
        cost_estimate=cost(),
        name="select_down",
    )(rows, stored)


def relative_columns(flip):
    size = lax.axis_size("tensor")
    me = lax.axis_index("tensor").astype(jnp.int32)
    chips = size // 2
    core = me % 2 if flip == 0 else 1 - me % 2
    return [(me // 2 + chips + shift) % chips * 2 + core for shift in SHIFTS]


def start_all(copies):
    for copy in copies:
        copy.start()
    return copies


def wait_all(copies):
    for copy in copies:
        copy.wait()


def base_product(tokens, value_matrix):
    rows, features = tokens.shape
    columns = value_matrix.shape[1]
    width = columns // lax.axis_size("tensor")
    chips = len(SHIFTS)
    steps = 4
    block = rows // steps

    def kernel(x_ref, v_ref, own_hbm, other_hbm, y_ref, out_sems):
        core = lax.axis_index("tensor").astype(jnp.int32) % 2
        spans = [pl.ds(step * block, block) for step in range(steps)]
        stores = []
        for step, span in enumerate(spans):
            product = dot(x_ref[span, :], v_ref[...], (1, 0)).astype(BF16)
            for index in range(2 * chips):
                y_ref[index % 2, index // 2, span, :] = product[:, index * width : (index + 1) * width]
            stores += start_all(
                [
                    pltpu.make_async_copy(y_ref.at[core, :, span], own_hbm.at[:, span], out_sems.at[0, step]),
                    pltpu.make_async_copy(y_ref.at[1 - core, :, span], other_hbm.at[:, span], out_sems.at[1, step]),
                ]
            )
        wait_all(stores)

    shape = pltpu.HBM((chips, rows, width), BF16)
    return pl.pallas_call(
        kernel,
        out_shape=(shape, shape),
        in_specs=[VMEM, VMEM],
        out_specs=(HBM, HBM),
        scratch_shapes=[
            pltpu.VMEM((2, chips, rows, width), BF16),
            pltpu.SemaphoreType.DMA((2, steps)),
        ],
        compiler_params=params(PART),
        cost_estimate=cost(),
        name="base_product",
    )(tokens, value_matrix)


def add_cores(own, other):
    chips, rows, width = own.shape

    def kernel(own_hbm, other_hbm, *refs):
        sums = refs[:chips]
        own_ref, other_ref, sum_ref, in_sems, out_sems = refs[chips:]
        mine = lax.axis_index("tensor").astype(jnp.int32) // 2
        fetch = []
        for index, shift in enumerate(SHIFTS):
            chip = (mine + chips + shift) % chips
            fetch += start_all(
                [
                    pltpu.make_async_copy(own_hbm.at[chip], own_ref.at[index], in_sems.at[0, index]),
                    pltpu.make_async_copy(other_hbm.at[chip], other_ref.at[index], in_sems.at[1, index]),
                ]
            )
        stores = []
        for index in range(chips):
            wait_all(fetch[2 * index : 2 * index + 2])
            sum_ref[index] = (own_ref[index].astype(F32) + other_ref[index].astype(F32)).astype(BF16)
            stores += start_all([pltpu.make_async_copy(sum_ref.at[index], sums[index], out_sems.at[index])])
        wait_all(stores)

    return pl.pallas_call(
        kernel,
        out_shape=[jax.ShapeDtypeStruct((rows, width), BF16)] * chips,
        in_specs=[HBM, HBM],
        out_specs=[ANY] * chips,
        scratch_shapes=[pltpu.VMEM(own.shape, BF16)] * 3
        + [pltpu.SemaphoreType.DMA((2, chips)), pltpu.SemaphoreType.DMA((chips,))],
        compiler_params=params(PART),
        cost_estimate=cost(),
        name="add_cores",
    )(in_hbm(own), in_hbm(other))


def back_product(holders, up, cotangent):
    tiles = holders.shape[0]

    def kernel(h_ref, up_ref, dy_ref, o_ref):
        for tile in range(tiles):
            o_ref[tile] = dot(
                up_ref[h_ref[tile]], dy_ref[tile * TILE : (tile + 1) * TILE, :], (1, 1)
            ).astype(BF16)

    return pl.pallas_call(
        kernel,
        out_shape=jax.ShapeDtypeStruct((tiles, up.shape[1], TILE), BF16),
        in_specs=[SMEM, VMEM, VMEM],
        out_specs=VMEM,
        compiler_params=params(PART),
        cost_estimate=cost(),
        name="back_product",
    )(holders, up, cotangent)


def low_product(holders, down, tokens):
    tiles = holders.shape[0]
    rank = down.shape[1]

    def kernel(h_ref, down_ref, x_ref, o_ref):
        for tile in range(tiles):
            o_ref[tile] = dot(
                down_ref[h_ref[tile]], x_ref[tile * TILE : (tile + 1) * TILE, :], (1, 1)
            ).astype(BF16)

    return pl.pallas_call(
        kernel,
        out_shape=jax.ShapeDtypeStruct((tiles, rank, TILE), BF16),
        in_specs=[SMEM, VMEM, VMEM],
        out_specs=VMEM,
        compiler_params=params(PART),
        cost_estimate=cost(1 << 40),
        name="low_product",
    )(holders, down, tokens)


def narrow_terms(holders, rank_side, wide_side, owners):
    tiles, rank, _ = rank_side.shape
    width = wide_side.shape[1]

    def kernel(h_ref, r_ref, w_ref, o_ref, total):
        total[...] = jnp.zeros_like(total)
        for tile in range(tiles):
            total[h_ref[tile]] += dot(r_ref[tile], w_ref[tile * TILE : (tile + 1) * TILE, :], (1, 0))
        o_ref[...] = (ADAPTER_SCALE * total[...]).astype(BF16)

    return pl.pallas_call(
        kernel,
        out_shape=jax.ShapeDtypeStruct((owners, rank, width), BF16),
        in_specs=[SMEM, VMEM, VMEM],
        out_specs=VMEM,
        scratch_shapes=[pltpu.VMEM((owners, rank, width), F32)],
        compiler_params=params(PART),
        cost_estimate=cost(),
        name="narrow_terms",
    )(holders, rank_side, wide_side)


def narrow_combine(rows, received, holding):
    users, rank, width = received.shape

    def kernel(rows_ref, r_ref, o_ref, total):
        total[...] = jnp.zeros_like(total)
        for user in range(users):

            @pl.when(rows_ref[user] >= 0)
            def _():
                total[jnp.maximum(rows_ref[user], 0)] += r_ref[user].astype(F32)

        o_ref[...] = total[...].astype(BF16)

    return pl.pallas_call(
        kernel,
        out_shape=jax.ShapeDtypeStruct((holding, rank, width), BF16),
        in_specs=[SMEM, VMEM],
        out_specs=VMEM,
        scratch_shapes=[pltpu.VMEM((holding, rank, width), F32)],
        compiler_params=params(PART),
        cost_estimate=cost(),
        name="narrow_combine",
    )(rows, received)


def gradient_terms(holders, rank_side, wide_side, owners):
    tiles, rank, _ = rank_side.shape
    width = wide_side.shape[1]
    parts = 4
    part = owners // parts

    def kernel(h_ref, r_ref, w_ref, o_hbm, total, o_ref, out_sems):
        total[...] = jnp.zeros_like(total)
        for tile in range(tiles):
            total[h_ref[tile]] += dot(r_ref[tile], w_ref[tile * TILE : (tile + 1) * TILE, :], (1, 0))
        stores = []
        for index in range(parts):
            span = pl.ds(index * part, part)
            o_ref[span] = (ADAPTER_SCALE * total[span]).astype(BF16)
            stores += start_all([pltpu.make_async_copy(o_ref.at[span], o_hbm.at[span], out_sems.at[index])])
        wait_all(stores)

    return pl.pallas_call(
        kernel,
        out_shape=pltpu.HBM((owners, rank, width), BF16),
        in_specs=[SMEM, VMEM, VMEM],
        out_specs=HBM,
        scratch_shapes=[
            pltpu.VMEM((owners, rank, width), F32),
            pltpu.VMEM((owners, rank, width), BF16),
            pltpu.SemaphoreType.DMA((parts,)),
        ],
        compiler_params=params(PART),
        cost_estimate=cost(),
        name="gradient_terms",
    )(holders, rank_side, wide_side)


def combine(rows, received, holding):
    users, rank, width = received.shape
    steps = 4
    part = rank // steps

    def kernel(rows_ref, r_hbm, o_hbm, r_ref, total, o_ref, in_sems, out_sems):
        spans = [pl.ds(step * part, part) for step in range(steps)]
        fetch = start_all(
            [
                pltpu.make_async_copy(r_hbm.at[:, span], r_ref.at[:, span], in_sems.at[step])
                for step, span in enumerate(spans)
            ]
        )
        stores = []
        for step, span in enumerate(spans):
            total[...] = jnp.zeros_like(total)
            fetch[step].wait()
            for user in range(users):

                @pl.when(rows_ref[user] >= 0)
                def _():
                    total[jnp.maximum(rows_ref[user], 0)] += r_ref[user, span].astype(F32)

            o_ref[:, span] = total[...].astype(BF16)
            stores += start_all([pltpu.make_async_copy(o_ref.at[:, span], o_hbm.at[:, span], out_sems.at[step])])
        wait_all(stores)

    return pl.pallas_call(
        kernel,
        out_shape=jax.ShapeDtypeStruct((holding, rank, width), BF16),
        in_specs=[SMEM, ANY],
        out_specs=HBM,
        scratch_shapes=[
            pltpu.VMEM(received.shape, BF16),
            pltpu.VMEM((holding, part, width), F32),
            pltpu.VMEM((holding, rank, width), BF16),
            pltpu.SemaphoreType.DMA((steps,)),
            pltpu.SemaphoreType.DMA((steps,)),
        ],
        compiler_params=params(PART),
        cost_estimate=cost(),
        name="combine",
    )(rows, received)


def finish_projected(holders, terms, lowrank, up):
    tiles = holders.shape[0]
    rows, width = terms[0].shape
    count = len(terms)
    middle = rows // 2

    def kernel(h_ref, *refs):
        l_hbm, up_hbm, o_hbm, t_ref, l_ref, up_ref, o_ref, term_sems, in_sems, out_sems = refs[count:]
        spans = [pl.ds(half * middle, middle) for half in range(2)]
        fetch = start_all(
            [
                pltpu.make_async_copy(source, target, in_sems.at[index])
                for index, (source, target) in enumerate(((l_hbm, l_ref), (up_hbm, up_ref)))
            ]
        )
        halves = [
            start_all(
                [
                    pltpu.make_async_copy(
                        refs[index].at[span], t_ref.at[index, span], term_sems.at[half, index]
                    )
                    for index in range(count)
                ]
            )
            for half, span in enumerate(spans)
        ]
        wait_all(fetch)
        stores = []
        for half, span in enumerate(spans):
            wait_all(halves[half])
            for tile in range(half * tiles // 2, (half + 1) * tiles // 2):
                rows_of = pl.ds(tile * TILE, TILE)
                total = ADAPTER_SCALE * dot(l_ref[tile], up_ref[h_ref[tile]], (0, 0))
                for index in range(count):
                    total = total + t_ref[index, rows_of, :].astype(F32)
                o_ref[rows_of, :] = total.astype(BF16)
            stores += start_all([pltpu.make_async_copy(o_ref.at[span], o_hbm.at[span], out_sems.at[half])])
        wait_all(stores)

    return pl.pallas_call(
        kernel,
        out_shape=jax.ShapeDtypeStruct((rows, width), BF16),
        in_specs=[SMEM] + [ANY] * (count + 2),
        out_specs=HBM,
        scratch_shapes=[
            pltpu.VMEM((count, rows, width), BF16),
            pltpu.VMEM(lowrank.shape, BF16),
            pltpu.VMEM(up.shape, BF16),
            pltpu.VMEM((rows, width), BF16),
            pltpu.SemaphoreType.DMA((2, count)),
            pltpu.SemaphoreType.DMA((2,)),
            pltpu.SemaphoreType.DMA((2,)),
        ],
        compiler_params=params(PART),
        cost_estimate=cost(),
        name="finish_projected",
    )(holders, *terms, lowrank, up)


def input_product(holders, pieces, value_matrix, back_low, down):
    rows, width = pieces[0].shape
    features, columns = value_matrix.shape
    steps = 4
    block = rows // steps
    group = block // TILE
    middle = rows // 2
    count = len(pieces)

    def kernel(h_ref, *refs):
        hbm = refs[:count]
        v_ref, b_ref, down_ref, o_hbm, dy_ref, o_ref, dy_sems, out_sems = refs[count:]
        halves = []
        for half in range(2):
            span = pl.ds(half * middle, middle)
            copies = []
            for flip in range(2):
                own, after_own, before_own, opposite = relative_columns(flip)
                own_hbm, left_hbm, right_hbm, first_hbm, last_hbm = hbm[flip * count // 2 : (flip + 1) * count // 2]
                sources = (
                    (own, own_hbm.at[span]),
                    (before_own, left_hbm.at[span]),
                    (after_own, right_hbm.at[span]),
                    (opposite, (first_hbm, last_hbm)[half]),
                )
                for index, (place, source) in enumerate(sources):
                    target = dy_ref.at[span, pl.ds(pl.multiple_of(place * width, width), width)]
                    copies.append(pltpu.make_async_copy(source, target, dy_sems.at[half, flip, index]))
            halves.append(copies)
        start_all(halves[0])
        stores = []
        for step in range(steps):
            if step == 0:
                wait_all(halves[0])
                start_all(halves[1])
            elif step * block == middle:
                wait_all(halves[1])
            span = pl.ds(step * block, block)
            frozen = dot(dy_ref[span, :], v_ref[...], (1, 1))
            for tile in range(group):
                adapter = dot(b_ref[step * group + tile], down_ref[h_ref[step * group + tile]], (0, 0))
                o_ref[pl.ds(step * block + tile * TILE, TILE), :] = (
                    frozen[tile * TILE : (tile + 1) * TILE, :] + ADAPTER_SCALE * adapter
                ).astype(BF16)
            stores += start_all([pltpu.make_async_copy(o_ref.at[span], o_hbm.at[span], out_sems.at[step])])
        wait_all(stores)

    return pl.pallas_call(
        kernel,
        out_shape=jax.ShapeDtypeStruct((rows, features), BF16),
        in_specs=[SMEM] + [HBM] * count + [VMEM] * 3,
        out_specs=HBM,
        scratch_shapes=[
            pltpu.VMEM((rows, columns), BF16),
            pltpu.VMEM((rows, features), BF16),
            pltpu.SemaphoreType.DMA((2, 2, 4)),
            pltpu.SemaphoreType.DMA((steps,)),
        ],
        compiler_params=params(PART),
        cost_estimate=cost(),
        name="input_product",
    )(holders, *map(in_hbm, pieces), value_matrix, back_low, down)


def swap_cores(array):
    size = lax.axis_size("tensor")
    return lax.ppermute(array, "tensor", [(i, i ^ 1) for i in range(size)])


def along_x(array, k):
    size = lax.axis_size("tensor")
    chips = size // 2
    return lax.ppermute(array, "tensor", [(i, (i // 2 + k) % chips * 2 + i % 2) for i in range(size)])


def sum_on_chip(part):
    return (part.astype(F32) + swap_cores(part).astype(F32)).astype(BF16)


def other_chips(own):
    return [along_x(own, shift) for shift in SHIFTS[1:]]


def sum_of(own, others):
    total = own.astype(F32)
    for other in others:
        total = total + other.astype(F32)
    return total.astype(BF16)


def shards(
    tokens,
    cotangent,
    value_matrix,
    down_factors,
    up_factors,
    tile_usage_entry,
    usage,
    storage_row_map,
):
    owners = lax.axis_size("dp")
    holding = down_factors.shape[0]
    down_stored = jnp.transpose(down_factors, (0, 2, 1))

    middle = cotangent.shape[0] // 2
    rows, holders, send_up = route_up(usage, storage_row_map, tile_usage_entry, up_factors, holding)
    up = lax.all_to_all(send_up, "dp", split_axis=0, concat_axis=0, tiled=True)
    left, right = along_x(cotangent, 1), along_x(cotangent, -1)
    send_down = after(select_rows(rows, down_stored), left, right)
    down = lax.all_to_all(send_down, "dp", split_axis=0, concat_axis=0, tiled=True)

    first, last = along_x(left[:middle], 1), along_x(right[middle:], -1)
    own_swapped = swap_cores(cotangent)
    back_part = back_product(holders, after(up, send_down, own_swapped), cotangent)
    left_swapped, right_swapped = swap_cores(left), swap_cores(right)
    back_chip = after(sum_on_chip(back_part), left_swapped, right_swapped)
    back_others = other_chips(back_chip)
    own_base, other_base = base_product(after(tokens, back_chip), value_matrix)
    first_swapped, last_swapped = swap_cores(first), swap_cores(last)
    back_others[2] = after(back_others[2], own_base, first, last)
    back_low = sum_of(back_chip, back_others)
    pieces = [cotangent, left, right, first, last]
    pieces += [own_swapped, left_swapped, right_swapped, first_swapped, last_swapped]
    sums = add_cores(own_base, swap_cores(other_base))
    frozen = [sums[0]] + [along_x(part, shift) for part, shift in zip(sums[1:], SHIFTS[1:])]
    send_down_terms = gradient_terms(holders, back_low, tokens, owners)
    down_terms = lax.all_to_all(send_down_terms, "dp", split_axis=0, concat_axis=0, tiled=True)

    low_chip = sum_on_chip(low_product(holders, after(down, send_down_terms), tokens))
    low_others = other_chips(low_chip)
    pieces[0] = after(pieces[0], low_chip)
    input_gradient = input_product(holders, pieces, value_matrix, back_low, down)
    low_others[2] = after(low_others[2], input_gradient)
    lowrank = sum_of(low_chip, low_others)
    send_up_terms = narrow_terms(holders, lowrank, cotangent, owners)
    down_terms, send_up_terms = lax.optimization_barrier((down_terms, send_up_terms))
    up_terms = lax.all_to_all(send_up_terms, "dp", split_axis=0, concat_axis=0, tiled=True)

    projected = finish_projected(holders, frozen, lowrank, up)
    up_gradient = narrow_combine(rows, after(up_terms, projected), holding)
    down_gradient = jnp.transpose(combine(rows, down_terms, holding), (0, 2, 1))
    return (projected, input_gradient, down_gradient, up_gradient)


def solution(mesh):
    return jax.shard_map(
        shards,
        mesh=mesh,
        in_specs=(
            P("dp", "tensor"),
            P("dp", "tensor"),
            P("tensor", None),
            P("dp", "tensor", None),
            P("dp", None, "tensor"),
            P("dp"),
            P(),
            P(),
        ),
        out_specs=(
            P("dp", "tensor"),
            P("dp", "tensor"),
            P("dp", "tensor", None),
            P("dp", None, "tensor"),
        ),
        check_vma=False,
    )
```

```python
import jax
import jax.numpy as jnp
from jax import lax
from jax.experimental import pallas as pl
from jax.experimental.pallas import tpu as pltpu
from jax.sharding import PartitionSpec as P

TILE = 128
ADAPTER_SCALE = 2.0
F32 = jnp.float32
BF16 = jnp.bfloat16
HBM = pl.BlockSpec(memory_space=pltpu.HBM)
ANY = pl.BlockSpec(memory_space=pl.ANY)
SMEM = pl.BlockSpec(memory_space=pltpu.SMEM)
VMEM = pl.BlockSpec(memory_space=pltpu.VMEM)
SHIFTS = (0, 1, -1, 2)
LIMIT = 62 * 1024 * 1024
PART = 24 * 1024 * 1024


def dot(a, b, contract):
    return lax.dot_general(a, b, ((contract[:1], contract[1:]), ((), ())), preferred_element_type=F32)


def cost(flops=1024):
    return pl.CostEstimate(flops=flops, bytes_accessed=1024, transcendentals=0)


def in_hbm(value):
    return pltpu.with_memory_space_constraint(value, pltpu.HBM)


def after(value, *others):
    return lax.optimization_barrier((value,) + others)[0]


def params(limit=LIMIT):
    return pltpu.CompilerParams(vmem_limit_bytes=limit)


def start_all(copies):
    for copy in copies:
        copy.start()
    return copies


def wait_all(copies):
    for copy in copies:
        copy.wait()


def pass_on(copies, held, target, sems):
    count = len(copies)
    onward = []
    for index, copy in enumerate(copies):
        copy.wait()
        onward.append(pltpu.make_async_copy(held.at[index], target.at[index], sems.at[count + index]))
        onward[-1].start()
    for copy in onward:
        copy.wait()


def route_up(usage, storage_row_map, entries, up, holding):
    users = lax.axis_size("dp")
    tiles = entries.shape[0]
    slots = usage.shape[0] // users

    def kernel(usage_hbm, map_hbm, entry_hbm, up_ref, rows_ref, holders_ref, send_ref, usage_ref, map_ref, entry_ref, held, sems, table_sems):
        tables = [
            pltpu.make_async_copy(source, target, table_sems.at[index])
            for index, (source, target) in enumerate(
                ((usage_hbm, usage_ref), (map_hbm, map_ref), (entry_hbm, entry_ref), (up_ref, held))
            )
        ]
        start_all(tables)
        wait_all(tables)
        mine = lax.axis_index("dp").astype(jnp.int32)
        copies = []
        for user in range(users):
            row = jnp.int32(-1)
            for slot in range(slots):
                place = map_ref[usage_ref[user * slots + slot]] - mine * holding
                row = jnp.where((place >= 0) & (place < holding), place, row)
            rows_ref[user] = row
            copies += start_all(
                [pltpu.make_async_copy(held.at[jnp.maximum(row, 0)], send_ref.at[user], sems.at[user])]
            )
        for tile in range(tiles):
            holders_ref[tile] = lax.div(map_ref[usage_ref[mine * slots + entry_ref[tile]]], jnp.int32(holding))
        wait_all(copies)

    return pl.pallas_call(
        kernel,
        out_shape=(
            jax.ShapeDtypeStruct((users,), jnp.int32),
            jax.ShapeDtypeStruct((tiles,), jnp.int32),
            jax.ShapeDtypeStruct((users,) + up.shape[1:], BF16),
        ),
        in_specs=[HBM, HBM, HBM, HBM],
        out_specs=(SMEM, SMEM, HBM),
        scratch_shapes=[
            pltpu.SMEM(usage.shape, jnp.int32),
            pltpu.SMEM(storage_row_map.shape, jnp.int32),
            pltpu.SMEM(entries.shape, jnp.int32),
            pltpu.VMEM(up.shape, BF16),
            pltpu.SemaphoreType.DMA((users,)),
            pltpu.SemaphoreType.DMA((4,)),
        ],
        compiler_params=params(),
        cost_estimate=cost(),
        name="route_up",
    )(usage, storage_row_map, entries, up)


def select_rows(rows, stored):
    users = rows.shape[0]

    def kernel(rows_ref, stored_ref, send_ref, held, sems):
        copies = []
        for user in range(users):
            row = jnp.maximum(rows_ref[user], 0)
            copies.append(pltpu.make_async_copy(stored_ref.at[row], held.at[user], sems.at[user]))
            copies[-1].start()
        pass_on(copies, held, send_ref, sems)

    return pl.pallas_call(
        kernel,
        out_shape=jax.ShapeDtypeStruct((users,) + stored.shape[1:], BF16),
        in_specs=[SMEM, HBM],
        out_specs=HBM,
        scratch_shapes=[
            pltpu.VMEM((users,) + stored.shape[1:], BF16),
            pltpu.SemaphoreType.DMA((2 * users,)),
        ],
        compiler_params=params(),
        cost_estimate=cost(),
        name="select_down",
    )(rows, stored)


def relative_columns(flip):
    size = lax.axis_size("tensor")
    me = lax.axis_index("tensor").astype(jnp.int32)
    chips = size // 2
    core = me % 2 if flip == 0 else 1 - me % 2
    return [(me // 2 + chips + shift) % chips * 2 + core for shift in SHIFTS]


def base_product(tokens, value_matrix):
    rows, features = tokens.shape
    columns = value_matrix.shape[1]
    width = columns // lax.axis_size("tensor")
    chips = len(SHIFTS)
    steps = 4
    block = rows // steps

    def kernel(x_ref, v_ref, own_hbm, other_hbm, y_ref, out_sems):
        core = lax.axis_index("tensor").astype(jnp.int32) % 2
        spans = [pl.ds(step * block, block) for step in range(steps)]
        stores = []
        for step, span in enumerate(spans):
            product = dot(x_ref[span, :], v_ref[...], (1, 0)).astype(BF16)
            for index in range(2 * chips):
                y_ref[index % 2, index // 2, span, :] = product[:, index * width : (index + 1) * width]
            stores += start_all(
                [
                    pltpu.make_async_copy(y_ref.at[core, :, span], own_hbm.at[:, span], out_sems.at[0, step]),
                    pltpu.make_async_copy(y_ref.at[1 - core, :, span], other_hbm.at[:, span], out_sems.at[1, step]),
                ]
            )
        wait_all(stores)

    shape = pltpu.HBM((chips, rows, width), BF16)
    return pl.pallas_call(
        kernel,
        out_shape=(shape, shape),
        in_specs=[VMEM, VMEM],
        out_specs=(HBM, HBM),
        scratch_shapes=[
            pltpu.VMEM((2, chips, rows, width), BF16),
            pltpu.SemaphoreType.DMA((2, steps)),
        ],
        compiler_params=params(PART),
        cost_estimate=cost(),
        name="base_product",
    )(tokens, value_matrix)


def add_cores(own, other):
    chips, rows, width = own.shape

    def kernel(own_hbm, other_hbm, *refs):
        sums = refs[:chips]
        own_ref, other_ref, sum_ref, in_sems, out_sems = refs[chips:]
        mine = lax.axis_index("tensor").astype(jnp.int32) // 2
        fetch = []
        for index, shift in enumerate(SHIFTS):
            chip = (mine + chips + shift) % chips
            fetch += start_all(
                [
                    pltpu.make_async_copy(own_hbm.at[chip], own_ref.at[index], in_sems.at[0, index]),
                    pltpu.make_async_copy(other_hbm.at[chip], other_ref.at[index], in_sems.at[1, index]),
                ]
            )
        stores = []
        for index in range(chips):
            wait_all(fetch[2 * index : 2 * index + 2])
            sum_ref[index] = (own_ref[index].astype(F32) + other_ref[index].astype(F32)).astype(BF16)
            stores += start_all([pltpu.make_async_copy(sum_ref.at[index], sums[index], out_sems.at[index])])
        wait_all(stores)

    return pl.pallas_call(
        kernel,
        out_shape=[jax.ShapeDtypeStruct((rows, width), BF16)] * chips,
        in_specs=[HBM, HBM],
        out_specs=[ANY] * chips,
        scratch_shapes=[pltpu.VMEM(own.shape, BF16)] * 3
        + [pltpu.SemaphoreType.DMA((2, chips)), pltpu.SemaphoreType.DMA((chips,))],
        compiler_params=params(PART),
        cost_estimate=cost(),
        name="add_cores",
    )(in_hbm(own), in_hbm(other))


def back_product(holders, up, cotangent):
    tiles = holders.shape[0]

    def kernel(h_ref, up_ref, dy_ref, o_ref):
        for tile in range(tiles):
            o_ref[tile] = dot(
                up_ref[h_ref[tile]], dy_ref[tile * TILE : (tile + 1) * TILE, :], (1, 1)
            ).astype(BF16)

    return pl.pallas_call(
        kernel,
        out_shape=jax.ShapeDtypeStruct((tiles, up.shape[1], TILE), BF16),
        in_specs=[SMEM, VMEM, VMEM],
        out_specs=VMEM,
        compiler_params=params(PART),
        cost_estimate=cost(),
        name="back_product",
    )(holders, up, cotangent)


def low_product(holders, down, tokens):
    tiles = holders.shape[0]
    rank = down.shape[1]

    def kernel(h_ref, down_ref, x_ref, o_ref):
        for tile in range(tiles):
            o_ref[tile] = dot(
                down_ref[h_ref[tile]], x_ref[tile * TILE : (tile + 1) * TILE, :], (1, 1)
            ).astype(BF16)

    return pl.pallas_call(
        kernel,
        out_shape=jax.ShapeDtypeStruct((tiles, rank, TILE), BF16),
        in_specs=[SMEM, VMEM, VMEM],
        out_specs=VMEM,
        compiler_params=params(PART),
        cost_estimate=cost(1 << 40),
        name="low_product",
    )(holders, down, tokens)


def narrow_terms(holders, rank_side, wide_side, owners):
    tiles, rank, _ = rank_side.shape
    width = wide_side.shape[1]

    def kernel(h_ref, r_ref, w_ref, o_ref, total):
        total[...] = jnp.zeros_like(total)
        for tile in range(tiles):
            total[h_ref[tile]] += dot(r_ref[tile], w_ref[tile * TILE : (tile + 1) * TILE, :], (1, 0))
        o_ref[...] = (ADAPTER_SCALE * total[...]).astype(BF16)

    return pl.pallas_call(
        kernel,
        out_shape=jax.ShapeDtypeStruct((owners, rank, width), BF16),
        in_specs=[SMEM, VMEM, VMEM],
        out_specs=VMEM,
        scratch_shapes=[pltpu.VMEM((owners, rank, width), F32)],
        compiler_params=params(PART),
        cost_estimate=cost(),
        name="narrow_terms",
    )(holders, rank_side, wide_side)


def narrow_combine(rows, received, holding):
    users, rank, width = received.shape

    def kernel(rows_ref, r_ref, o_ref, total):
        total[...] = jnp.zeros_like(total)
        for user in range(users):

            @pl.when(rows_ref[user] >= 0)
            def _():
                total[jnp.maximum(rows_ref[user], 0)] += r_ref[user].astype(F32)

        o_ref[...] = total[...].astype(BF16)

    return pl.pallas_call(
        kernel,
        out_shape=jax.ShapeDtypeStruct((holding, rank, width), BF16),
        in_specs=[SMEM, VMEM],
        out_specs=VMEM,
        scratch_shapes=[pltpu.VMEM((holding, rank, width), F32)],
        compiler_params=params(PART),
        cost_estimate=cost(),
        name="narrow_combine",
    )(rows, received)


def gradient_terms(holders, rank_side, wide_side, owners):
    tiles, rank, _ = rank_side.shape
    width = wide_side.shape[1]
    parts = 4
    part = owners // parts

    def kernel(h_ref, r_ref, w_ref, o_hbm, total, o_ref, out_sems):
        total[...] = jnp.zeros_like(total)
        for tile in range(tiles):
            total[h_ref[tile]] += dot(r_ref[tile], w_ref[tile * TILE : (tile + 1) * TILE, :], (1, 0))
        stores = []
        for index in range(parts):
            span = pl.ds(index * part, part)
            o_ref[span] = (ADAPTER_SCALE * total[span]).astype(BF16)
            stores += start_all([pltpu.make_async_copy(o_ref.at[span], o_hbm.at[span], out_sems.at[index])])
        wait_all(stores)

    return pl.pallas_call(
        kernel,
        out_shape=pltpu.HBM((owners, rank, width), BF16),
        in_specs=[SMEM, VMEM, VMEM],
        out_specs=HBM,
        scratch_shapes=[
            pltpu.VMEM((owners, rank, width), F32),
            pltpu.VMEM((owners, rank, width), BF16),
            pltpu.SemaphoreType.DMA((parts,)),
        ],
        compiler_params=params(PART),
        cost_estimate=cost(),
        name="gradient_terms",
    )(holders, rank_side, wide_side)


def combine(rows, received, holding):
    users, rank, width = received.shape
    steps = 4
    part = rank // steps

    def kernel(rows_ref, r_hbm, o_hbm, r_ref, total, o_ref, in_sems, out_sems):
        spans = [pl.ds(step * part, part) for step in range(steps)]
        fetch = start_all(
            [
                pltpu.make_async_copy(r_hbm.at[:, span], r_ref.at[:, span], in_sems.at[step])
                for step, span in enumerate(spans)
            ]
        )
        stores = []
        for step, span in enumerate(spans):
            total[...] = jnp.zeros_like(total)
            fetch[step].wait()
            for user in range(users):

                @pl.when(rows_ref[user] >= 0)
                def _():
                    total[jnp.maximum(rows_ref[user], 0)] += r_ref[user, span].astype(F32)

            o_ref[:, span] = total[...].astype(BF16)
            stores += start_all([pltpu.make_async_copy(o_ref.at[:, span], o_hbm.at[:, span], out_sems.at[step])])
        wait_all(stores)

    return pl.pallas_call(
        kernel,
        out_shape=jax.ShapeDtypeStruct((holding, rank, width), BF16),
        in_specs=[SMEM, ANY],
        out_specs=HBM,
        scratch_shapes=[
            pltpu.VMEM(received.shape, BF16),
            pltpu.VMEM((holding, part, width), F32),
            pltpu.VMEM((holding, rank, width), BF16),
            pltpu.SemaphoreType.DMA((steps,)),
            pltpu.SemaphoreType.DMA((steps,)),
        ],
        compiler_params=params(PART),
        cost_estimate=cost(),
        name="combine",
    )(rows, received)


def finish_projected(holders, terms, lowrank, up):
    tiles = holders.shape[0]
    rows, width = terms[0].shape
    count = len(terms)
    middle = rows // 2

    def kernel(h_ref, *refs):
        l_hbm, up_hbm, o_hbm, t_ref, l_ref, up_ref, o_ref, term_sems, in_sems, out_sems = refs[count:]
        spans = [pl.ds(half * middle, middle) for half in range(2)]
        fetch = start_all(
            [
                pltpu.make_async_copy(source, target, in_sems.at[index])
                for index, (source, target) in enumerate(((l_hbm, l_ref), (up_hbm, up_ref)))
            ]
        )
        halves = [
            start_all(
                [
                    pltpu.make_async_copy(
                        refs[index].at[span], t_ref.at[index, span], term_sems.at[half, index]
                    )
                    for index in range(count)
                ]
            )
            for half, span in enumerate(spans)
        ]
        wait_all(fetch)
        stores = []
        for half, span in enumerate(spans):
            wait_all(halves[half])
            for tile in range(half * tiles // 2, (half + 1) * tiles // 2):
                rows_of = pl.ds(tile * TILE, TILE)
                total = ADAPTER_SCALE * dot(l_ref[tile], up_ref[h_ref[tile]], (0, 0))
                for index in range(count):
                    total = total + t_ref[index, rows_of, :].astype(F32)
                o_ref[rows_of, :] = total.astype(BF16)
            stores += start_all([pltpu.make_async_copy(o_ref.at[span], o_hbm.at[span], out_sems.at[half])])
        wait_all(stores)

    return pl.pallas_call(
        kernel,
        out_shape=jax.ShapeDtypeStruct((rows, width), BF16),
        in_specs=[SMEM] + [ANY] * (count + 2),
        out_specs=HBM,
        scratch_shapes=[
            pltpu.VMEM((count, rows, width), BF16),
            pltpu.VMEM(lowrank.shape, BF16),
            pltpu.VMEM(up.shape, BF16),
            pltpu.VMEM((rows, width), BF16),
            pltpu.SemaphoreType.DMA((2, count)),
            pltpu.SemaphoreType.DMA((2,)),
            pltpu.SemaphoreType.DMA((2,)),
        ],
        compiler_params=params(PART),
        cost_estimate=cost(),
        name="finish_projected",
    )(holders, *terms, lowrank, up)


def input_product(holders, pieces, value_matrix, back_low, down):
    rows, width = pieces[0].shape
    features, columns = value_matrix.shape
    steps = 4
    block = rows // steps
    group = block // TILE
    middle = rows // 2
    count = len(pieces)

    def kernel(h_ref, *refs):
        hbm = refs[:count]
        v_ref, b_ref, down_ref, o_hbm, dy_ref, o_ref, dy_sems, out_sems = refs[count:]
        halves = []
        for half in range(2):
            span = pl.ds(half * middle, middle)
            copies = []
            for flip in range(2):
                own, after_own, before_own, opposite = relative_columns(flip)
                own_hbm, left_hbm, right_hbm, first_hbm, last_hbm = hbm[flip * count // 2 : (flip + 1) * count // 2]
                sources = (
                    (own, own_hbm.at[span]),
                    (before_own, left_hbm.at[span]),
                    (after_own, right_hbm.at[span]),
                    (opposite, (first_hbm, last_hbm)[half]),
                )
                for index, (place, source) in enumerate(sources):
                    target = dy_ref.at[span, pl.ds(pl.multiple_of(place * width, width), width)]
                    copies.append(pltpu.make_async_copy(source, target, dy_sems.at[half, flip, index]))
            halves.append(copies)
        start_all(halves[0])
        stores = []
        for step in range(steps):
            if step == 0:
                wait_all(halves[0])
                start_all(halves[1])
            elif step * block == middle:
                wait_all(halves[1])
            span = pl.ds(step * block, block)
            frozen = dot(dy_ref[span, :], v_ref[...], (1, 1))
            for tile in range(group):
                adapter = dot(b_ref[step * group + tile], down_ref[h_ref[step * group + tile]], (0, 0))
                o_ref[pl.ds(step * block + tile * TILE, TILE), :] = (
                    frozen[tile * TILE : (tile + 1) * TILE, :] + ADAPTER_SCALE * adapter
                ).astype(BF16)
            stores += start_all([pltpu.make_async_copy(o_ref.at[span], o_hbm.at[span], out_sems.at[step])])
        wait_all(stores)

    return pl.pallas_call(
        kernel,
        out_shape=jax.ShapeDtypeStruct((rows, features), BF16),
        in_specs=[SMEM] + [HBM] * count + [VMEM] * 3,
        out_specs=HBM,
        scratch_shapes=[
            pltpu.VMEM((rows, columns), BF16),
            pltpu.VMEM((rows, features), BF16),
            pltpu.SemaphoreType.DMA((2, 2, 4)),
            pltpu.SemaphoreType.DMA((steps,)),
        ],
        compiler_params=params(PART),
        cost_estimate=cost(),
        name="input_product",
    )(holders, *map(in_hbm, pieces), value_matrix, back_low, down)


def swap_cores(array):
    size = lax.axis_size("tensor")
    return lax.ppermute(array, "tensor", [(i, i ^ 1) for i in range(size)])


def along_x(array, k):
    size = lax.axis_size("tensor")
    chips = size // 2
    return lax.ppermute(array, "tensor", [(i, (i // 2 + k) % chips * 2 + i % 2) for i in range(size)])


def sum_on_chip(part):
    return (part.astype(F32) + swap_cores(part).astype(F32)).astype(BF16)


def other_chips(own):
    return [along_x(own, shift) for shift in SHIFTS[1:]]


def sum_of(own, others):
    total = own.astype(F32)
    for other in others:
        total = total + other.astype(F32)
    return total.astype(BF16)


def shards(
    tokens,
    cotangent,
    value_matrix,
    down_factors,
    up_factors,
    tile_usage_entry,
    usage,
    storage_row_map,
):
    owners = lax.axis_size("dp")
    holding = down_factors.shape[0]
    down_stored = jnp.transpose(down_factors, (0, 2, 1))

    middle = cotangent.shape[0] // 2
    rows, holders, send_up = route_up(usage, storage_row_map, tile_usage_entry, up_factors, holding)
    up = lax.all_to_all(send_up, "dp", split_axis=0, concat_axis=0, tiled=True)
    left, right = along_x(cotangent, 1), along_x(cotangent, -1)
    send_down = after(select_rows(rows, down_stored), left, right)
    down = lax.all_to_all(send_down, "dp", split_axis=0, concat_axis=0, tiled=True)

    first, last = along_x(left[:middle], 1), along_x(right[middle:], -1)
    own_swapped = swap_cores(cotangent)
    back_part = back_product(holders, after(up, send_down), cotangent)
    left_swapped, right_swapped = swap_cores(left), swap_cores(right)
    back_chip = after(sum_on_chip(back_part), own_swapped, left_swapped, right_swapped)
    back_others = other_chips(back_chip)
    own_base, other_base = base_product(after(tokens, back_chip), value_matrix)
    first_swapped, last_swapped = swap_cores(first), swap_cores(last)
    back_others[2] = after(back_others[2], own_base)
    back_low = sum_of(back_chip, back_others)
    pieces = [cotangent, left, right, first, last]
    pieces += [own_swapped, left_swapped, right_swapped, first_swapped, last_swapped]
    sums = add_cores(own_base, swap_cores(other_base))
    frozen = [sums[0]] + [along_x(part, shift) for part, shift in zip(sums[1:], SHIFTS[1:])]
    send_down_terms = gradient_terms(holders, back_low, tokens, owners)
    down_terms = lax.all_to_all(send_down_terms, "dp", split_axis=0, concat_axis=0, tiled=True)

    low_chip = after(sum_on_chip(low_product(holders, after(down, send_down_terms), tokens)), first, last)
    low_others = other_chips(low_chip)
    pieces[0] = after(pieces[0], low_chip)
    input_gradient = input_product(holders, pieces, value_matrix, back_low, down)
    low_others[2] = after(low_others[2], input_gradient)
    lowrank = sum_of(low_chip, low_others)
    send_up_terms = narrow_terms(holders, lowrank, cotangent, owners)
    down_terms, send_up_terms = lax.optimization_barrier((down_terms, send_up_terms))
    up_terms = lax.all_to_all(send_up_terms, "dp", split_axis=0, concat_axis=0, tiled=True)

    projected = finish_projected(holders, frozen, lowrank, up)
    up_gradient = narrow_combine(rows, after(up_terms, projected), holding)
    down_gradient = jnp.transpose(combine(rows, down_terms, holding), (0, 2, 1))
    return (projected, input_gradient, down_gradient, up_gradient)


def solution(mesh):
    return jax.shard_map(
        shards,
        mesh=mesh,
        in_specs=(
            P("dp", "tensor"),
            P("dp", "tensor"),
            P("tensor", None),
            P("dp", "tensor", None),
            P("dp", None, "tensor"),
            P("dp"),
            P(),
            P(),
        ),
        out_specs=(
            P("dp", "tensor"),
            P("dp", "tensor"),
            P("dp", "tensor", None),
            P("dp", None, "tensor"),
        ),
        check_vma=False,
    )
```

```python
import jax
import jax.numpy as jnp
from jax import lax
from jax.experimental import pallas as pl
from jax.experimental.pallas import tpu as pltpu
from jax.sharding import PartitionSpec as P

TILE = 128
ADAPTER_SCALE = 2.0
F32 = jnp.float32
BF16 = jnp.bfloat16
HBM = pl.BlockSpec(memory_space=pltpu.HBM)
ANY = pl.BlockSpec(memory_space=pl.ANY)
SMEM = pl.BlockSpec(memory_space=pltpu.SMEM)
VMEM = pl.BlockSpec(memory_space=pltpu.VMEM)
SHIFTS = (0, 1, -1, 2)
LIMIT = 62 * 1024 * 1024
PART = 24 * 1024 * 1024


def dot(a, b, contract):
    return lax.dot_general(a, b, ((contract[:1], contract[1:]), ((), ())), preferred_element_type=F32)


def cost(flops=1024):
    return pl.CostEstimate(flops=flops, bytes_accessed=1024, transcendentals=0)


def in_hbm(value):
    return pltpu.with_memory_space_constraint(value, pltpu.HBM)


def after(value, *others):
    return lax.optimization_barrier((value,) + others)[0]


def params(limit=LIMIT):
    return pltpu.CompilerParams(vmem_limit_bytes=limit)


def start_all(copies):
    for copy in copies:
        copy.start()
    return copies


def wait_all(copies):
    for copy in copies:
        copy.wait()


def pass_on(copies, held, target, sems):
    count = len(copies)
    onward = []
    for index, copy in enumerate(copies):
        copy.wait()
        onward.append(pltpu.make_async_copy(held.at[index], target.at[index], sems.at[count + index]))
        onward[-1].start()
    for copy in onward:
        copy.wait()


def route_up(usage, storage_row_map, entries, up, holding):
    users = lax.axis_size("dp")
    tiles = entries.shape[0]
    slots = usage.shape[0] // users

    def kernel(usage_hbm, map_hbm, entry_hbm, up_ref, rows_ref, holders_ref, send_ref, usage_ref, map_ref, entry_ref, held, sems, table_sems):
        tables = [
            pltpu.make_async_copy(source, target, table_sems.at[index])
            for index, (source, target) in enumerate(
                ((usage_hbm, usage_ref), (map_hbm, map_ref), (entry_hbm, entry_ref), (up_ref, held))
            )
        ]
        start_all(tables)
        wait_all(tables)
        mine = lax.axis_index("dp").astype(jnp.int32)
        copies = []
        for user in range(users):
            row = jnp.int32(-1)
            for slot in range(slots):
                place = map_ref[usage_ref[user * slots + slot]] - mine * holding
                row = jnp.where((place >= 0) & (place < holding), place, row)
            rows_ref[user] = row
            copies += start_all(
                [pltpu.make_async_copy(held.at[jnp.maximum(row, 0)], send_ref.at[user], sems.at[user])]
            )
        for tile in range(tiles):
            holders_ref[tile] = lax.div(map_ref[usage_ref[mine * slots + entry_ref[tile]]], jnp.int32(holding))
        wait_all(copies)

    return pl.pallas_call(
        kernel,
        out_shape=(
            jax.ShapeDtypeStruct((users,), jnp.int32),
            jax.ShapeDtypeStruct((tiles,), jnp.int32),
            jax.ShapeDtypeStruct((users,) + up.shape[1:], BF16),
        ),
        in_specs=[HBM, HBM, HBM, HBM],
        out_specs=(SMEM, SMEM, HBM),
        scratch_shapes=[
            pltpu.SMEM(usage.shape, jnp.int32),
            pltpu.SMEM(storage_row_map.shape, jnp.int32),
            pltpu.SMEM(entries.shape, jnp.int32),
            pltpu.VMEM(up.shape, BF16),
            pltpu.SemaphoreType.DMA((users,)),
            pltpu.SemaphoreType.DMA((4,)),
        ],
        compiler_params=params(),
        cost_estimate=cost(),
        name="route_up",
    )(usage, storage_row_map, entries, up)


def select_rows(rows, stored):
    users = rows.shape[0]

    def kernel(rows_ref, stored_ref, send_ref, held, sems):
        copies = []
        for user in range(users):
            row = jnp.maximum(rows_ref[user], 0)
            copies.append(pltpu.make_async_copy(stored_ref.at[row], held.at[user], sems.at[user]))
            copies[-1].start()
        pass_on(copies, held, send_ref, sems)

    return pl.pallas_call(
        kernel,
        out_shape=jax.ShapeDtypeStruct((users,) + stored.shape[1:], BF16),
        in_specs=[SMEM, HBM],
        out_specs=HBM,
        scratch_shapes=[
            pltpu.VMEM((users,) + stored.shape[1:], BF16),
            pltpu.SemaphoreType.DMA((2 * users,)),
        ],
        compiler_params=params(),
        cost_estimate=cost(),
        name="select_down",
    )(rows, stored)


def relative_columns(flip):
    size = lax.axis_size("tensor")
    me = lax.axis_index("tensor").astype(jnp.int32)
    chips = size // 2
    core = me % 2 if flip == 0 else 1 - me % 2
    return [(me // 2 + chips + shift) % chips * 2 + core for shift in SHIFTS]


def base_product(tokens, value_matrix):
    rows, features = tokens.shape
    columns = value_matrix.shape[1]
    width = columns // lax.axis_size("tensor")
    chips = len(SHIFTS)
    steps = 4
    block = rows // steps

    def kernel(x_ref, v_ref, own_hbm, other_hbm, y_ref, out_sems):
        core = lax.axis_index("tensor").astype(jnp.int32) % 2
        spans = [pl.ds(step * block, block) for step in range(steps)]
        stores = []
        for step, span in enumerate(spans):
            product = dot(x_ref[span, :], v_ref[...], (1, 0)).astype(BF16)
            for index in range(2 * chips):
                y_ref[index % 2, index // 2, span, :] = product[:, index * width : (index + 1) * width]
            stores += start_all(
                [
                    pltpu.make_async_copy(y_ref.at[core, :, span], own_hbm.at[:, span], out_sems.at[0, step]),
                    pltpu.make_async_copy(y_ref.at[1 - core, :, span], other_hbm.at[:, span], out_sems.at[1, step]),
                ]
            )
        wait_all(stores)

    shape = pltpu.HBM((chips, rows, width), BF16)
    return pl.pallas_call(
        kernel,
        out_shape=(shape, shape),
        in_specs=[VMEM, VMEM],
        out_specs=(HBM, HBM),
        scratch_shapes=[
            pltpu.VMEM((2, chips, rows, width), BF16),
            pltpu.SemaphoreType.DMA((2, steps)),
        ],
        compiler_params=params(PART),
        cost_estimate=cost(),
        name="base_product",
    )(tokens, value_matrix)


def add_cores(own, other):
    chips, rows, width = own.shape

    def kernel(own_hbm, other_hbm, *refs):
        sums = refs[:chips]
        own_ref, other_ref, sum_ref, in_sems, out_sems = refs[chips:]
        mine = lax.axis_index("tensor").astype(jnp.int32) // 2
        fetch = []
        for index, shift in enumerate(SHIFTS):
            chip = (mine + chips + shift) % chips
            fetch += start_all(
                [
                    pltpu.make_async_copy(own_hbm.at[chip], own_ref.at[index], in_sems.at[0, index]),
                    pltpu.make_async_copy(other_hbm.at[chip], other_ref.at[index], in_sems.at[1, index]),
                ]
            )
        stores = []
        for index in range(chips):
            wait_all(fetch[2 * index : 2 * index + 2])
            sum_ref[index] = (own_ref[index].astype(F32) + other_ref[index].astype(F32)).astype(BF16)
            stores += start_all([pltpu.make_async_copy(sum_ref.at[index], sums[index], out_sems.at[index])])
        wait_all(stores)

    return pl.pallas_call(
        kernel,
        out_shape=[jax.ShapeDtypeStruct((rows, width), BF16)] * chips,
        in_specs=[HBM, HBM],
        out_specs=[ANY] * chips,
        scratch_shapes=[pltpu.VMEM(own.shape, BF16)] * 3
        + [pltpu.SemaphoreType.DMA((2, chips)), pltpu.SemaphoreType.DMA((chips,))],
        compiler_params=params(PART),
        cost_estimate=cost(),
        name="add_cores",
    )(in_hbm(own), in_hbm(other))


def back_product(holders, up, cotangent):
    tiles = holders.shape[0]

    def kernel(h_ref, up_ref, dy_ref, o_ref):
        for tile in range(tiles):
            o_ref[tile] = dot(
                up_ref[h_ref[tile]], dy_ref[tile * TILE : (tile + 1) * TILE, :], (1, 1)
            ).astype(BF16)

    return pl.pallas_call(
        kernel,
        out_shape=jax.ShapeDtypeStruct((tiles, up.shape[1], TILE), BF16),
        in_specs=[SMEM, VMEM, VMEM],
        out_specs=VMEM,
        compiler_params=params(PART),
        cost_estimate=cost(),
        name="back_product",
    )(holders, up, cotangent)


def low_product(holders, down, tokens):
    tiles = holders.shape[0]
    rank = down.shape[1]

    def kernel(h_ref, down_ref, x_ref, o_ref):
        for tile in range(tiles):
            o_ref[tile] = dot(
                down_ref[h_ref[tile]], x_ref[tile * TILE : (tile + 1) * TILE, :], (1, 1)
            ).astype(BF16)

    return pl.pallas_call(
        kernel,
        out_shape=jax.ShapeDtypeStruct((tiles, rank, TILE), BF16),
        in_specs=[SMEM, VMEM, VMEM],
        out_specs=VMEM,
        compiler_params=params(PART),
        cost_estimate=cost(1 << 40),
        name="low_product",
    )(holders, down, tokens)


def narrow_terms(holders, rank_side, wide_side, owners):
    tiles, rank, _ = rank_side.shape
    width = wide_side.shape[1]

    def kernel(h_ref, r_ref, w_ref, o_ref, total):
        total[...] = jnp.zeros_like(total)
        for tile in range(tiles):
            total[h_ref[tile]] += dot(r_ref[tile], w_ref[tile * TILE : (tile + 1) * TILE, :], (1, 0))
        o_ref[...] = (ADAPTER_SCALE * total[...]).astype(BF16)

    return pl.pallas_call(
        kernel,
        out_shape=jax.ShapeDtypeStruct((owners, rank, width), BF16),
        in_specs=[SMEM, VMEM, VMEM],
        out_specs=VMEM,
        scratch_shapes=[pltpu.VMEM((owners, rank, width), F32)],
        compiler_params=params(PART),
        cost_estimate=cost(),
        name="narrow_terms",
    )(holders, rank_side, wide_side)


def narrow_combine(rows, received, holding):
    users, rank, width = received.shape

    def kernel(rows_ref, r_ref, o_ref, total):
        total[...] = jnp.zeros_like(total)
        for user in range(users):

            @pl.when(rows_ref[user] >= 0)
            def _():
                total[jnp.maximum(rows_ref[user], 0)] += r_ref[user].astype(F32)

        o_ref[...] = total[...].astype(BF16)

    return pl.pallas_call(
        kernel,
        out_shape=jax.ShapeDtypeStruct((holding, rank, width), BF16),
        in_specs=[SMEM, VMEM],
        out_specs=VMEM,
        scratch_shapes=[pltpu.VMEM((holding, rank, width), F32)],
        compiler_params=params(PART),
        cost_estimate=cost(),
        name="narrow_combine",
    )(rows, received)


def gradient_terms(holders, rank_side, wide_side, owners):
    tiles, rank, _ = rank_side.shape
    width = wide_side.shape[1]
    parts = 4
    part = owners // parts

    def kernel(h_ref, r_ref, w_ref, o_hbm, total, o_ref, out_sems):
        total[...] = jnp.zeros_like(total)
        for tile in range(tiles):
            total[h_ref[tile]] += dot(r_ref[tile], w_ref[tile * TILE : (tile + 1) * TILE, :], (1, 0))
        stores = []
        for index in range(parts):
            span = pl.ds(index * part, part)
            o_ref[span] = (ADAPTER_SCALE * total[span]).astype(BF16)
            stores += start_all([pltpu.make_async_copy(o_ref.at[span], o_hbm.at[span], out_sems.at[index])])
        wait_all(stores)

    return pl.pallas_call(
        kernel,
        out_shape=pltpu.HBM((owners, rank, width), BF16),
        in_specs=[SMEM, VMEM, VMEM],
        out_specs=HBM,
        scratch_shapes=[
            pltpu.VMEM((owners, rank, width), F32),
            pltpu.VMEM((owners, rank, width), BF16),
            pltpu.SemaphoreType.DMA((parts,)),
        ],
        compiler_params=params(PART),
        cost_estimate=cost(),
        name="gradient_terms",
    )(holders, rank_side, wide_side)


def combine(rows, received, holding):
    users, rank, width = received.shape
    steps = 4
    part = rank // steps

    def kernel(rows_ref, r_hbm, o_hbm, r_ref, total, o_ref, in_sems, out_sems):
        spans = [pl.ds(step * part, part) for step in range(steps)]
        fetch = start_all(
            [
                pltpu.make_async_copy(r_hbm.at[:, span], r_ref.at[:, span], in_sems.at[step])
                for step, span in enumerate(spans)
            ]
        )
        stores = []
        for step, span in enumerate(spans):
            total[...] = jnp.zeros_like(total)
            fetch[step].wait()
            for user in range(users):

                @pl.when(rows_ref[user] >= 0)
                def _():
                    total[jnp.maximum(rows_ref[user], 0)] += r_ref[user, span].astype(F32)

            o_ref[:, span] = total[...].astype(BF16)
            stores += start_all([pltpu.make_async_copy(o_ref.at[:, span], o_hbm.at[:, span], out_sems.at[step])])
        wait_all(stores)

    return pl.pallas_call(
        kernel,
        out_shape=jax.ShapeDtypeStruct((holding, rank, width), BF16),
        in_specs=[SMEM, ANY],
        out_specs=HBM,
        scratch_shapes=[
            pltpu.VMEM(received.shape, BF16),
            pltpu.VMEM((holding, part, width), F32),
            pltpu.VMEM((holding, rank, width), BF16),
            pltpu.SemaphoreType.DMA((steps,)),
            pltpu.SemaphoreType.DMA((steps,)),
        ],
        compiler_params=params(PART),
        cost_estimate=cost(),
        name="combine",
    )(rows, received)


def finish_projected(holders, terms, lowrank, up):
    tiles = holders.shape[0]
    rows, width = terms[0].shape
    count = len(terms)

    def kernel(h_ref, l_ref, up_ref, *refs):
        for tile in range(tiles):
            span = pl.ds(tile * TILE, TILE)
            total = ADAPTER_SCALE * dot(l_ref[tile], up_ref[h_ref[tile]], (0, 0))
            for ref in refs[:count]:
                total = total + ref[span, :].astype(F32)
            refs[count][span, :] = total.astype(BF16)

    return pl.pallas_call(
        kernel,
        out_shape=jax.ShapeDtypeStruct((rows, width), BF16),
        in_specs=[SMEM] + [VMEM] * (count + 2),
        out_specs=VMEM,
        compiler_params=params(PART),
        cost_estimate=cost(),
        name="finish_projected",
    )(holders, lowrank, up, *terms)


def input_product(holders, pieces, value_matrix, back_low, down):
    rows, width = pieces[0].shape
    features, columns = value_matrix.shape
    steps = 4
    block = rows // steps
    group = block // TILE
    middle = rows // 2
    count = len(pieces)

    def kernel(h_ref, *refs):
        hbm = refs[:count]
        v_ref, b_ref, down_ref, o_hbm, dy_ref, o_ref, dy_sems, out_sems = refs[count:]
        halves = []
        for half in range(2):
            span = pl.ds(half * middle, middle)
            copies = []
            for flip in range(2):
                own, after_own, before_own, opposite = relative_columns(flip)
                own_hbm, left_hbm, right_hbm, first_hbm, last_hbm = hbm[flip * count // 2 : (flip + 1) * count // 2]
                sources = (
                    (own, own_hbm.at[span]),
                    (before_own, left_hbm.at[span]),
                    (after_own, right_hbm.at[span]),
                    (opposite, (first_hbm, last_hbm)[half]),
                )
                for index, (place, source) in enumerate(sources):
                    target = dy_ref.at[span, pl.ds(pl.multiple_of(place * width, width), width)]
                    copies.append(pltpu.make_async_copy(source, target, dy_sems.at[half, flip, index]))
            halves.append(copies)
        start_all(halves[0])
        stores = []
        for step in range(steps):
            if step == 0:
                wait_all(halves[0])
                start_all(halves[1])
            elif step * block == middle:
                wait_all(halves[1])
            span = pl.ds(step * block, block)
            frozen = dot(dy_ref[span, :], v_ref[...], (1, 1))
            for tile in range(group):
                adapter = dot(b_ref[step * group + tile], down_ref[h_ref[step * group + tile]], (0, 0))
                o_ref[pl.ds(step * block + tile * TILE, TILE), :] = (
                    frozen[tile * TILE : (tile + 1) * TILE, :] + ADAPTER_SCALE * adapter
                ).astype(BF16)
            stores += start_all([pltpu.make_async_copy(o_ref.at[span], o_hbm.at[span], out_sems.at[step])])
        wait_all(stores)

    return pl.pallas_call(
        kernel,
        out_shape=jax.ShapeDtypeStruct((rows, features), BF16),
        in_specs=[SMEM] + [HBM] * count + [VMEM] * 3,
        out_specs=HBM,
        scratch_shapes=[
            pltpu.VMEM((rows, columns), BF16),
            pltpu.VMEM((rows, features), BF16),
            pltpu.SemaphoreType.DMA((2, 2, 4)),
            pltpu.SemaphoreType.DMA((steps,)),
        ],
        compiler_params=params(PART),
        cost_estimate=cost(),
        name="input_product",
    )(holders, *map(in_hbm, pieces), value_matrix, back_low, down)


def swap_cores(array):
    size = lax.axis_size("tensor")
    return lax.ppermute(array, "tensor", [(i, i ^ 1) for i in range(size)])


def along_x(array, k):
    size = lax.axis_size("tensor")
    chips = size // 2
    return lax.ppermute(array, "tensor", [(i, (i // 2 + k) % chips * 2 + i % 2) for i in range(size)])


def sum_on_chip(part):
    return (part.astype(F32) + swap_cores(part).astype(F32)).astype(BF16)


def other_chips(own):
    return [along_x(own, shift) for shift in SHIFTS[1:]]


def sum_of(own, others):
    total = own.astype(F32)
    for other in others:
        total = total + other.astype(F32)
    return total.astype(BF16)


def shards(
    tokens,
    cotangent,
    value_matrix,
    down_factors,
    up_factors,
    tile_usage_entry,
    usage,
    storage_row_map,
):
    owners = lax.axis_size("dp")
    holding = down_factors.shape[0]
    down_stored = jnp.transpose(down_factors, (0, 2, 1))

    middle = cotangent.shape[0] // 2
    rows, holders, send_up = route_up(usage, storage_row_map, tile_usage_entry, up_factors, holding)
    up = lax.all_to_all(send_up, "dp", split_axis=0, concat_axis=0, tiled=True)
    left, right = along_x(cotangent, 1), along_x(cotangent, -1)
    send_down = after(select_rows(rows, down_stored), left, right)
    down = lax.all_to_all(send_down, "dp", split_axis=0, concat_axis=0, tiled=True)

    first, last = along_x(left[:middle], 1), along_x(right[middle:], -1)
    own_swapped = swap_cores(cotangent)
    back_part = back_product(holders, after(up, send_down), cotangent)
    left_swapped, right_swapped = swap_cores(left), swap_cores(right)
    back_chip = after(sum_on_chip(back_part), own_swapped, left_swapped, right_swapped)
    back_others = other_chips(back_chip)
    own_base, other_base = base_product(after(tokens, back_chip), value_matrix)
    first_swapped, last_swapped = swap_cores(first), swap_cores(last)
    back_others[2] = after(back_others[2], own_base)
    back_low = sum_of(back_chip, back_others)
    pieces = [cotangent, left, right, first, last]
    pieces += [own_swapped, left_swapped, right_swapped, first_swapped, last_swapped]
    sums = add_cores(own_base, swap_cores(other_base))
    frozen = [sums[0]] + [along_x(part, shift) for part, shift in zip(sums[1:], SHIFTS[1:])]
    send_down_terms = gradient_terms(holders, back_low, tokens, owners)
    down_terms = lax.all_to_all(send_down_terms, "dp", split_axis=0, concat_axis=0, tiled=True)

    low_chip = after(sum_on_chip(low_product(holders, after(down, send_down_terms), tokens)), first, last)
    low_others = other_chips(low_chip)
    pieces[0] = after(pieces[0], low_chip)
    input_gradient = input_product(holders, pieces, value_matrix, back_low, down)
    low_others[2] = after(low_others[2], input_gradient)
    lowrank = sum_of(low_chip, low_others)
    send_up_terms = narrow_terms(holders, lowrank, cotangent, owners)
    down_terms, send_up_terms = lax.optimization_barrier((down_terms, send_up_terms))
    up_terms = lax.all_to_all(send_up_terms, "dp", split_axis=0, concat_axis=0, tiled=True)

    projected = finish_projected(holders, frozen, lowrank, up)
    up_gradient = narrow_combine(rows, after(up_terms, projected), holding)
    down_gradient = jnp.transpose(combine(rows, down_terms, holding), (0, 2, 1))
    return (projected, input_gradient, down_gradient, up_gradient)


def solution(mesh):
    return jax.shard_map(
        shards,
        mesh=mesh,
        in_specs=(
            P("dp", "tensor"),
            P("dp", "tensor"),
            P("tensor", None),
            P("dp", "tensor", None),
            P("dp", None, "tensor"),
            P("dp"),
            P(),
            P(),
        ),
        out_specs=(
            P("dp", "tensor"),
            P("dp", "tensor"),
            P("dp", "tensor", None),
            P("dp", None, "tensor"),
        ),
        check_vma=False,
    )
```
